256 devices in a mesh: replica: 16 (over x_lo, y, core), fsdp: 16 (over z, x_hi).
Axes of the slice: x: 4 (x_hi: 2, x_lo: 2; x = x_hi * 2 + x_lo), y: 4, z: 8, core: 2. Of those that a mesh axis runs over, the one named last changes fastest.
Arguments:
- tokens: bfloat16 [65536, 8192], P(('replica', 'fsdp')), may hold values from -6 to 6
- weight: bfloat16 [8192, 1024], P('fsdp'), may hold values from -0.0625 to 0.0625
- momentum: float32 [16, 8192, 1024], P('replica', 'fsdp'), may hold values from -6 to 6
- gradient: bfloat16 [16, 8192, 1024], P('replica', 'fsdp'), may hold values from -6 to 6
- indices: int32 [16, 128, 16, 32], P('replica', 'fsdp'), may hold values from 0 to 4095, as said below
Outputs:
- keys: bfloat16 [65536, 1024], P(('replica', 'fsdp'))
- new_weight: bfloat16 [8192, 1024], P('fsdp')
- new_momentum: float32 [16, 8192, 1024], P('replica', 'fsdp')
The draws below stay inside these ranges and needn't reach their ends.
Inputs may be any that keep to these rules, and one draw needn't show every extreme that they name: `indices`: within each group of each replica the 32 positions differ; a position is row * 64 + column in the group's coefficient block.
All inputs are finite; a program needn't handle non-finite values.
Results may differ from the reference program's by a relative error of at most 0.0049.
Values may be sent and summed in bfloat16 or wider, within the bound.
A program may use at most 128 MiB of HBM per device.

```python
import jax
import jax.numpy as jnp
from jax import lax

D = 8192
KV = 1024
BLOCK = 64
K = 32
REPLICAS = 16
TOKENS = 65536


def draw_indices(key, part):
    key = jax.random.fold_in(key, 5)
    square = BLOCK * BLOCK
    subkeys = jax.random.split(key, REPLICAS * (D // BLOCK))

    def one_line(sub):
        scores = jax.random.randint(sub, (KV // BLOCK, square), 0, 2 ** 18) * square
        scores = scores + jnp.arange(square, dtype=jnp.int32)[None, :]
        chosen = lax.top_k(scores, K)[1]
        return chosen.astype(jnp.int32)
    picks = lax.map(one_line, subkeys)
    return picks.reshape(REPLICAS, D // BLOCK, KV // BLOCK, K).astype(jnp.int32)


def levels(own_key, shape, cuts, low, high):
    factor_of = 1.0
    for dim, parts in cuts:
        steps = jax.random.uniform(jax.random.fold_in(jax.random.fold_in(own_key, 6), dim), (parts,), jnp.float32, low / len(cuts), high / len(cuts))
        factor_of = factor_of * jnp.repeat(jnp.exp(steps), shape[dim] // parts).reshape((-1,) + (1,) * (len(shape) - 1 - dim))
    return factor_of


def centred(rng, shape, spread, reach, cuts=(), held_as=jnp.bfloat16):
    array = spread * jax.random.normal(rng, shape, jnp.float32)
    if cuts:
        array = array * levels(rng, shape, cuts, -0.22, 0.18)
    return jnp.clip(array, -reach, reach).astype(held_as)


def setup_inputs(seed: int = 0) -> dict:
    key_of = jax.random.split(jax.random.key(seed), 6)
    tokens = centred(key_of[0], (TOKENS, D), 1.0, 6.0, ((0, 256),))
    weight = centred(key_of[1], (D, KV), D ** -0.5, 0.0625, ((0, 16),))
    momentum = centred(key_of[2], (REPLICAS, D, KV), 1.0, 6.0, ((0, 16), (1, 16)), jnp.float32)
    gradient = centred(key_of[3], (REPLICAS, D, KV), 1.0, 6.0, ((0, 16), (1, 16)))
    indices = draw_indices(jax.random.fold_in(key_of[5], 71), 0)
    return dict(tokens=tokens, weight=weight, momentum=momentum, gradient=gradient, indices=indices)


momentum_decay = 0.9
step_size = 0.1

def dct_table(size):
    freq = jnp.arange(size, dtype=jnp.float32)[:, None]
    place = jnp.arange(size, dtype=jnp.float32)[None, :]
    scale = jnp.where(freq == 0, jnp.sqrt(1.0 / size), jnp.sqrt(2.0 / size))
    return scale * jnp.cos(jnp.pi * (2.0 * place + 1.0) * freq / (2.0 * size))

def forward_dct(blocks, table):
    inner = jnp.einsum('ki,xiyj->xkyj', table, blocks, precision=lax.Precision.HIGHEST)
    return jnp.einsum('xkyj,lj->xkyl', inner, table, precision=lax.Precision.HIGHEST)

def inverse_dct(coeffs, table):
    inner = jnp.einsum('ki,xkyl->xiyl', table, coeffs, precision=lax.Precision.HIGHEST)
    return jnp.einsum('xiyl,lj->xiyj', inner, table, precision=lax.Precision.HIGHEST)

def one_hot(values, size):
    return (values[..., None] == jnp.arange(size, dtype=jnp.int32)).astype(jnp.float32)

def reference(tokens, weight, momentum, gradient, indices):
    table = dct_table(BLOCK)
    group_rows = D // BLOCK
    group_cols = KV // BLOCK

    def per_replica(args):
        mom, grad, places = args
        moved = momentum_decay * mom + grad.astype(jnp.float32)
        blocks = moved.reshape(group_rows, BLOCK, group_cols, BLOCK)
        coeffs = forward_dct(blocks, table)
        row_hot = one_hot(places // BLOCK, BLOCK)
        col_hot = one_hot(places % BLOCK, BLOCK)
        partial_rows = jnp.einsum('xytk,xkyl->xytl', row_hot, coeffs, precision=lax.Precision.HIGHEST)
        picked = lax.optimization_barrier(jnp.sum(partial_rows * col_hot, axis=-1))
        own = jnp.einsum('xyt,xytk,xytl->xkyl', picked, row_hot, col_hot, precision=lax.Precision.HIGHEST)
        fresh = moved - inverse_dct(own, table).reshape(D, KV)
        return (fresh, picked)
    new_momentum, picked = lax.map(per_replica, (momentum, gradient, indices))

    def one_row(args):
        values, places = args
        row_hot = one_hot(places // BLOCK, BLOCK)
        col_hot = one_hot(places % BLOCK, BLOCK)
        return jnp.einsum('ryt,rytk,rytl->kyl', values, row_hot, col_hot, precision=lax.Precision.HIGHEST)
    total = lax.map(one_row, (jnp.transpose(picked, (1, 0, 2, 3)), jnp.transpose(indices, (1, 0, 2, 3))))
    update = inverse_dct(total, table).reshape(D, KV) / REPLICAS
    new_weight = (weight.astype(jnp.float32) - step_size * update).astype(jnp.bfloat16)
    keys = jnp.dot(tokens, new_weight, preferred_element_type=jnp.float32).astype(jnp.bfloat16)
    return (keys, new_weight, new_momentum)
```

```python
import functools

import jax
import jax.numpy as jnp
import ml_dtypes
import numpy as np
from jax import lax
from jax.experimental import pallas as pl
from jax.experimental.pallas import tpu as pltpu
from jax.sharding import PartitionSpec as P

BLOCK = 64
K = 32
QUAD = 256
MESH = pl.DeviceIdType.MESH
F32 = jnp.float32
BF16 = jnp.bfloat16

momentum_decay = 0.9
step_size = 0.1


def dct_table(size):
    freq = np.arange(size, dtype=np.float64)[:, None]
    place = np.arange(size, dtype=np.float64)[None, :]
    scale = np.where(freq == 0, np.sqrt(1.0 / size), np.sqrt(2.0 / size))
    return (scale * np.cos(np.pi * (2.0 * place + 1.0) * freq / (2.0 * size))).astype(np.float32)


def tables():
    table = dct_table(BLOCK)
    high = table.astype(ml_dtypes.bfloat16)
    low = (table - high.astype(np.float32)).astype(ml_dtypes.bfloat16)
    stacked = np.concatenate([high.T, low.T], axis=0)
    across = np.kron(np.eye(4, dtype=np.float32), table)
    return stacked, table.T.copy(), across


def split(value):
    high = value.astype(BF16)
    return high, (value - high.astype(F32)).astype(BF16)


def dot_tn(a, b):
    return lax.dot_general(a, b, (((0,), (0,)), ((), ())), preferred_element_type=F32)


def dot_nt(a, b):
    return lax.dot_general(a, b, (((1,), (1,)), ((), ())), preferred_element_type=F32)


def pick_kernel(stacked_ref, momentum_ref, gradient_ref, indices_ref, packed_ref, fresh_ref):
    group_rows = momentum_ref.shape[0] // BLOCK
    quads = momentum_ref.shape[1] // QUAD
    lanes = lax.broadcasted_iota(jnp.int32, (BLOCK, 128), 1) // K
    freq = lax.broadcasted_iota(jnp.int32, (BLOCK, 128), 0)
    for x in range(group_rows):
        rows = pl.ds(x * BLOCK, BLOCK)
        for quad in range(quads):
            columns = pl.ds(quad * QUAD, QUAD)
            moved = momentum_decay * momentum_ref[rows, columns] + gradient_ref[rows, columns].astype(F32)
            place = indices_ref[x, quad : quad + 1, :]
            hot = jnp.concatenate(
                [
                    jnp.where(freq == place // BLOCK, 1.0, 0.0).astype(BF16),
                    jnp.where(freq == place % BLOCK, 1.0, 0.0).astype(BF16),
                ],
                axis=1,
            )
            chosen = jnp.dot(stacked_ref[...], hot, preferred_element_type=F32)
            row_high, row_low = chosen[:BLOCK, :128], chosen[BLOCK:, :128]
            col_high, col_low = chosen[:BLOCK, 128:], chosen[BLOCK:, 128:]
            row_wave, col_wave = row_high + row_low, col_high + col_low
            moved_high, moved_low = split(moved)
            partial = dot_tn(
                jnp.concatenate([moved_high, moved_low, moved_high], axis=0),
                jnp.concatenate([row_high, row_high, row_low], axis=0).astype(BF16),
            )
            mine = jnp.where(lanes == 0, partial[:BLOCK], 0.0)
            for part in range(1, 4):
                mine = jnp.where(lanes == part, partial[part * BLOCK : (part + 1) * BLOCK], mine)
            picked = jnp.sum(mine * col_wave, axis=0, keepdims=True)
            packet = x * 2 + quad // 2
            packed_ref[packet, quad % 2 : quad % 2 + 1, :] = picked
            packed_ref[packet, 2 + quad % 2 : 3 + quad % 2, :] = place.astype(F32)
            own_high, own_low = split(row_wave * picked)
            spread_high = jnp.concatenate([jnp.where(lanes == i, col_high, 0.0) for i in range(4)], axis=0).astype(BF16)
            spread_low = jnp.concatenate([jnp.where(lanes == i, col_low, 0.0) for i in range(4)], axis=0).astype(BF16)
            back = dot_nt(
                jnp.concatenate([own_high, own_high, own_low], axis=1),
                jnp.concatenate([spread_high, spread_low, spread_high], axis=1),
            )
            fresh_ref[rows, columns] = moved - back


def pick(momentum, gradient, indices, stacked):
    rows, width = momentum.shape
    steps = 4
    tall = rows // steps
    groups = tall // BLOCK
    return pl.pallas_call(
        pick_kernel,
        grid=(steps,),
        in_specs=[
            pl.BlockSpec(stacked.shape, lambda i: (0, 0)),
            pl.BlockSpec((tall, width), lambda i: (i, 0)),
            pl.BlockSpec((tall, width), lambda i: (i, 0)),
            pl.BlockSpec((groups, 4, 128), lambda i: (i, 0, 0)),
        ],
        out_specs=[
            pl.BlockSpec((groups * 2, 8, 128), lambda i: (i, 0, 0)),
            pl.BlockSpec((tall, width), lambda i: (i, 0)),
        ],
        out_shape=[
            jax.ShapeDtypeStruct((16, 8, 128), F32),
            jax.ShapeDtypeStruct((rows, width), F32),
        ],
        compiler_params=pltpu.CompilerParams(vmem_limit_bytes=48 * 2**20),
    )(stacked, momentum, gradient, indices)


def apply_kernel(
    turn_ref,
    across_ref,
    packed_ref,
    weight_ref,
    tokens_ref,
    keys_ref,
    fresh_ref,
    tokens_all,
    weight_mine,
    got,
    big,
    mid,
    small,
    total_acc,
    local_sem,
    send_sem,
    recv_sem,
):
    r, f = lax.axis_index("replica"), lax.axis_index("fsdp")
    x = lax.rem(f, 2) * 2 + r // 8
    y = lax.rem(r // 2, 4)
    z = f // 2
    c = lax.rem(r, 2)
    p, q = x + c * (y - x), y + c * (x - y)

    def device(p, q, z, c=c):
        x, y = p + c * (q - p), q + c * (p - q)
        return (lax.rem(x, 2) * 8 + y * 2 + c, z * 2 + x // 2)

    def around(value, step, size):
        return lax.rem(value + step + size, size)

    sibling = (r + 1 - 2 * c, f)
    z_peers = [(d, device(p, q, around(z, d, 8))) for d in range(1, 8)]
    p_peers = [(d, device(around(p, d, 4), q, z)) for d in range(1, 4)]
    q_peers = [(d, device(p, around(q, d, 4), z)) for d in range(1, 4)]
    group = [(d, (lax.rem(r + d, 16), f)) for d in range(1, 16)]
    x_far = [(lax.rem(r + d, 16), f + 1 - 2 * lax.rem(f, 2)) for d in (0, 8)]

    barrier = pltpu.get_barrier_semaphore()
    others = [peer for _, peer in z_peers + group] + x_far
    for peer in others:
        pl.semaphore_signal(barrier, inc=1, device_id=peer, device_id_type=MESH)
    pl.semaphore_wait(barrier, len(others))

    started = []
    count = [0]

    def lane():
        count[0] += 1
        return count[0] - 1

    def send(src, dst, slot, peer):
        copy = pltpu.make_async_remote_copy(
            src_ref=src,
            dst_ref=dst,
            send_sem=send_sem.at[slot],
            recv_sem=recv_sem.at[slot],
            device_id=peer,
            device_id_type=MESH,
        )
        copy.start()
        started.append(copy)

    def receive(dst, slot):
        pltpu.make_async_remote_copy(
            src_ref=dst,
            dst_ref=dst,
            send_sem=send_sem.at[slot],
            recv_sem=recv_sem.at[slot],
            device_id=sibling,
            device_id_type=MESH,
        ).wait_recv()

    group_slots = [lane() for _ in group]
    for (d, peer), slot in zip(group, group_slots):
        send(packed_ref.at[peer[0]], got.at[r], slot, peer)
    own_copy = pltpu.make_async_copy(packed_ref.at[r], got.at[r], local_sem.at[0])
    own_copy.start()
    g = lax.rem(x, 2) * 4 + y
    weight_copy = pltpu.make_async_copy(
        weight_ref.at[pl.ds(pl.multiple_of(g * BLOCK, BLOCK), BLOCK), pl.ds(pl.multiple_of(c * 512, 512), 512)],
        weight_mine,
        local_sem.at[1],
    )
    weight_copy.start()
    token_slot = lane()
    tokens_copy = pltpu.make_async_copy(tokens_ref, tokens_all.at[c], local_sem.at[2])
    tokens_copy.start()
    send(tokens_ref, tokens_all.at[c], token_slot, sibling)

    own_copy.wait()
    weight_copy.wait()
    for (d, peer), slot in zip(group, group_slots):
        receive(got.at[around(r, -d, 16)], slot)

    freq = lax.broadcasted_iota(jnp.int32, (BLOCK, 128), 0)
    wide = lax.broadcasted_iota(jnp.int32, (QUAD, 128), 0)
    offset = (lax.broadcasted_iota(jnp.int32, (1, 128), 1) // K) * BLOCK
    fresh = []
    for unit in range(2):
        high, low, hot = [], [], []
        for source in range(16):
            value = got[source, unit : unit + 1, :]
            place = got[source, 2 + unit : 3 + unit, :].astype(jnp.int32)
            here = freq == place // BLOCK
            value_high, value_low = split(value)
            high.append(jnp.where(here, value_high.astype(F32), 0.0).astype(BF16))
            low.append(jnp.where(here, value_low.astype(F32), 0.0).astype(BF16))
            hot.append(jnp.where(wide == place % BLOCK + offset, 1.0, 0.0).astype(BF16))
        left = jnp.concatenate([jnp.concatenate(high, axis=1), jnp.concatenate(low, axis=1)], axis=0)
        both = dot_nt(left, jnp.concatenate(hot, axis=1))
        total = both[:BLOCK] + both[BLOCK:]
        inner = jnp.dot(turn_ref[...], total, precision=lax.Precision.HIGHEST, preferred_element_type=F32)
        update = jnp.dot(inner, across_ref[...], precision=lax.Precision.HIGHEST, preferred_element_type=F32) / 16.0
        old = weight_mine[:, unit * QUAD : (unit + 1) * QUAD].astype(F32)
        fresh.append((old - step_size * update).astype(BF16))
    big[q, p, z] = fresh[0]
    mid[p, q, z] = fresh[1][:, :128]
    small[z, q, p] = fresh[1][:, 128:]

    small_1 = [lane() for _ in p_peers]
    mid_1 = [lane() for _ in z_peers]
    big_1 = [lane() for _ in z_peers]
    for (d, peer), slot in zip(p_peers, small_1):
        send(small.at[z, q, p], small.at[z, q, p], slot, peer)
    for (d, peer), slot in zip(z_peers, mid_1):
        send(mid.at[p, q, z], mid.at[p, q, z], slot, peer)
    for (d, peer), slot in zip(z_peers, big_1):
        send(big.at[q, p, z], big.at[q, p, z], slot, peer)

    p_next, p_last = p_peers[0][1], p_peers[2][1]
    q_next, q_last = q_peers[0][1], q_peers[2][1]
    z_next, z_last = z_peers[0][1], z_peers[6][1]
    small_2 = [lane() for _ in q_peers]
    mid_2 = [lane() for _ in q_peers]
    big_2 = [lane() for _ in p_peers]
    mid_3 = [(lane(), lane()) for _ in range(4)]
    big_3 = [(lane(), lane()) for _ in range(4)]
    mid_4 = [lane() for _ in range(4)]
    big_4 = [lane() for _ in range(4)]
    small_3 = [[(lane(), lane()) for _ in range(2)] for _ in range(4)]

    for (d, peer), slot in zip(p_peers, small_1):
        receive(small.at[z, q, around(p, -d, 4)], slot)
    for (d, peer), slot in zip(q_peers, small_2):
        send(small.at[z, q], small.at[z, q], slot, peer)

    for (d, peer), slot in zip(z_peers, mid_1):
        receive(mid.at[p, q, around(z, -d, 8)], slot)
    for (d, peer), slot in zip(q_peers, mid_2):
        send(mid.at[p, q], mid.at[p, q], slot, peer)
    send(mid.at[p, q], mid.at[p, q], mid_3[0][0], p_next)
    send(mid.at[p, q], mid.at[p, q], mid_3[0][1], p_last)

    for (d, peer), slot in zip(z_peers, big_1):
        receive(big.at[q, p, around(z, -d, 8)], slot)
    for (d, peer), slot in zip(p_peers, big_2):
        send(big.at[q, p], big.at[q, p], slot, peer)
    send(big.at[q, p], big.at[q, p], big_3[0][0], q_next)
    send(big.at[q, p], big.at[q, p], big_3[0][1], q_last)

    for (d, peer), slot in zip(q_peers, small_2):
        receive(small.at[z, around(q, -d, 4)], slot)
    halves = [pl.ds(0, 2), pl.ds(2, 2)]
    for half in range(2):
        send(small.at[z, halves[half]], small.at[z, halves[half]], small_3[0][half][0], z_next)
        send(small.at[z, halves[half]], small.at[z, halves[half]], small_3[0][half][1], z_last)

    for d in (1, 3, 2):
        here = mid.at[p, around(q, -d, 4)]
        receive(here, mid_2[d - 1])
        send(here, here, mid_3[d][0], p_next)
        send(here, here, mid_3[d][1], p_last)
        here = big.at[q, around(p, -d, 4)]
        receive(here, big_2[d - 1])
        send(here, here, big_3[d][0], q_next)
        send(here, here, big_3[d][1], q_last)

    def small_step(step):
        before, after = around(z, -step, 8), around(z, step, 8)
        for half in range(2):
            receive(small.at[before, halves[half]], small_3[step - 1][half][0])
            if step < 3 or half == 0:
                here = small.at[before, halves[half]]
                send(here, here, small_3[step][half][0], z_next)
            receive(small.at[after, halves[half]], small_3[step - 1][half][1])
            if step < 3 or half == 1:
                here = small.at[after, halves[half]]
                send(here, here, small_3[step][half][1], z_last)

    for turn, d in enumerate((0, 1, 3, 2)):
        for buffer, slots, onward, first, second, ahead, behind in (
            (mid, mid_3, mid_4, p, q, p_next, p_last),
            (big, big_3, big_4, q, p, q_next, q_last),
        ):
            sub = around(second, -d, 4)
            left = buffer.at[around(first, -1, 4), sub]
            right = buffer.at[around(first, 1, 4), sub]
            receive(left, slots[d][0])
            if d in (0, 2):
                send(left, left, onward[d], ahead)
            receive(right, slots[d][1])
            if d in (1, 3):
                send(right, right, onward[d], behind)
        if turn < 3:
            small_step(turn + 1)

    opposite = around(z, 4, 8)
    for d in (0, 1, 3, 2):
        receive(mid.at[around(p, 2, 4), around(q, -d, 4)], mid_4[d])
        receive(big.at[around(q, 2, 4), around(p, -d, 4)], big_4[d])
    receive(small.at[opposite, halves[0]], small_3[3][0][0])
    receive(small.at[opposite, halves[1]], small_3[3][1][1])

    weight_slot = lane()
    keys_slot = lane()

    def rows_of(zi, xi, yi):
        pi, qi = xi + c * (yi - xi), yi + c * (xi - yi)
        return jnp.concatenate([big[qi, pi, zi], mid[pi, qi, zi], small[zi, qi, pi]], axis=1)

    x_high = 2 * lax.rem(f, 2)
    for xi in range(2):
        for yi in range(4):
            fresh_ref[c, xi * 4 + yi] = rows_of(z, x_high + xi, yi)
    send(fresh_ref.at[c], fresh_ref.at[c], weight_slot, sibling)

    tokens_copy.wait()
    receive(tokens_all.at[1 - c], token_slot)
    total_acc[...] = jnp.zeros_like(total_acc)

    def multiply(zi, carry):
        right = jnp.concatenate([rows_of(zi, xi, yi) for xi in range(4) for yi in range(4)], axis=0)
        depth = pl.ds(pl.multiple_of(zi * 1024, 1024), 1024)
        for half in range(2):
            total_acc[half] += jnp.dot(tokens_all[half, :, depth], right, preferred_element_type=F32)
        return carry

    lax.fori_loop(0, 8, multiply, 0)
    keys_ref[c] = total_acc[c].astype(BF16)
    got_keys = total_acc[1 - c].astype(BF16)
    tokens_all[0, :, :512] = got_keys
    send(tokens_all.at[0, :, pl.ds(0, 512)], keys_ref.at[c], keys_slot, sibling)
    receive(fresh_ref.at[1 - c], weight_slot)
    receive(keys_ref.at[1 - c], keys_slot)
    for copy in started:
        copy.wait_send()


def apply(packed, weight, tokens, turn, across):
    vmem = pl.BlockSpec(memory_space=pltpu.VMEM)
    hbm = pl.BlockSpec(memory_space=pl.ANY)
    slots = 128
    return pl.pallas_call(
        apply_kernel,
        in_specs=[vmem, vmem, vmem, hbm, hbm],
        out_specs=[vmem, vmem],
        out_shape=[
            jax.ShapeDtypeStruct((2, 256, 512), BF16),
            jax.ShapeDtypeStruct((2, 8, 64, 512), BF16),
        ],
        scratch_shapes=[
            pltpu.VMEM((2, 256, 8192), BF16),
            pltpu.VMEM((64, 512), BF16),
            pltpu.VMEM((16, 8, 128), F32),
            pltpu.VMEM((4, 4, 8, 64, 256), BF16),
            pltpu.VMEM((4, 4, 8, 64, 128), BF16),
            pltpu.VMEM((8, 4, 4, 64, 128), BF16),
            pltpu.VMEM((2, 256, 512), F32),
            pltpu.SemaphoreType.DMA((3,)),
            pltpu.SemaphoreType.DMA((slots,)),
            pltpu.SemaphoreType.DMA((slots,)),
        ],
        compiler_params=pltpu.CompilerParams(collective_id=0, has_side_effects=True, vmem_limit_bytes=56 * 2**20),
    )(turn, across, packed, weight, tokens)


def per_device(tokens, weight, momentum, gradient, indices):
    stacked, turn, across = tables()
    packed, new_momentum = pick(momentum[0], gradient[0], indices.reshape(8, 4, 128), jnp.asarray(stacked))
    keys, fresh = apply(packed, weight, tokens, jnp.asarray(turn), jnp.asarray(across))
    keys = jnp.transpose(keys, (1, 0, 2)).reshape(tokens.shape[0], weight.shape[1])
    fresh = jnp.transpose(fresh.reshape(2, weight.shape[0], 512), (1, 0, 2)).reshape(weight.shape)
    return (keys, fresh, new_momentum[None])


def solution(mesh):
    return jax.shard_map(
        per_device,
        mesh=mesh,
        in_specs=(
            P(("replica", "fsdp"), None),
            P("fsdp", None),
            P("replica", "fsdp", None),
            P("replica", "fsdp", None),
            P("replica", "fsdp", None, None),
        ),
        out_specs=(P(("replica", "fsdp"), None), P("fsdp", None), P("replica", "fsdp", None)),
        check_vma=False,
    )
```

```python
import functools

import jax
import jax.numpy as jnp
import ml_dtypes
import numpy as np
from jax import lax
from jax.experimental import pallas as pl
from jax.experimental.pallas import tpu as pltpu
from jax.sharding import PartitionSpec as P

BLOCK = 64
K = 32
QUAD = 256
MESH = pl.DeviceIdType.MESH
F32 = jnp.float32
BF16 = jnp.bfloat16

momentum_decay = 0.9
step_size = 0.1


def dct_table(size):
    freq = np.arange(size, dtype=np.float64)[:, None]
    place = np.arange(size, dtype=np.float64)[None, :]
    scale = np.where(freq == 0, np.sqrt(1.0 / size), np.sqrt(2.0 / size))
    return (scale * np.cos(np.pi * (2.0 * place + 1.0) * freq / (2.0 * size))).astype(np.float32)


def tables():
    table = dct_table(BLOCK)
    high = table.astype(ml_dtypes.bfloat16)
    low = (table - high.astype(np.float32)).astype(ml_dtypes.bfloat16)
    out = np.zeros((192, 768), ml_dtypes.bfloat16)
    out[:64, :192] = np.concatenate([high, high, low], axis=1)
    out[64:128, 256:512] = np.tile(high, (1, 4))
    out[64:128, 512:768] = np.tile(low, (1, 4))
    out[128:, :192] = np.concatenate([high.T, high.T, low.T], axis=1)
    return out


def split(value):
    high = value.astype(BF16)
    return high, (value - high.astype(F32)).astype(BF16)


def dot_tn(a, b):
    return lax.dot_general(a, b, (((0,), (0,)), ((), ())), preferred_element_type=F32)


def dot_nt(a, b):
    return lax.dot_general(a, b, (((1,), (1,)), ((), ())), preferred_element_type=F32)


def step_kernel(
    table_ref,
    indices_ref,
    momentum_ref,
    gradient_ref,
    weight_ref,
    tokens_ref,
    keys_ref,
    fresh_ref,
    moment_ref,
    table,
    moment,
    slope,
    waves,
    picks,
    packed,
    tokens_all,
    weight_mine,
    got,
    big,
    mid,
    small,
    total_acc,
    local_sem,
    load_sem,
    send_sem,
    recv_sem,
):
    r, f = lax.axis_index("replica"), lax.axis_index("fsdp")
    x = lax.rem(f, 2) * 2 + r // 8
    y = lax.rem(r // 2, 4)
    z = f // 2
    c = lax.rem(r, 2)
    p, q = x + c * (y - x), y + c * (x - y)

    def device(p, q, z, c=c):
        x, y = p + c * (q - p), q + c * (p - q)
        return (lax.rem(x, 2) * 8 + y * 2 + c, z * 2 + x // 2)

    def around(value, step, size):
        return lax.rem(value + step + size, size)

    sibling = (r + 1 - 2 * c, f)
    z_peers = [(d, device(p, q, around(z, d, 8))) for d in range(1, 8)]
    p_peers = [(d, device(around(p, d, 4), q, z)) for d in range(1, 4)]
    q_peers = [(d, device(p, around(q, d, 4), z)) for d in range(1, 4)]
    group = [(d, (lax.rem(r + d, 16), f)) for d in range(1, 16)]
    x_far = [(lax.rem(r + d, 16), f + 1 - 2 * lax.rem(f, 2)) for d in (0, 8)]

    barrier = pltpu.get_barrier_semaphore()
    others = [peer for _, peer in z_peers + group] + x_far
    for peer in others:
        pl.semaphore_signal(barrier, inc=1, device_id=peer, device_id_type=MESH)

    started, whole = [], []
    count = [0]

    def lane():
        count[0] += 1
        return count[0] - 1

    def send(src, dst, slot, peer, keep=True):
        copy = pltpu.make_async_remote_copy(
            src_ref=src,
            dst_ref=dst,
            send_sem=send_sem.at[slot],
            recv_sem=recv_sem.at[slot],
            device_id=peer,
            device_id_type=MESH,
        )
        copy.start()
        if keep:
            started.append(copy)

    def receive(dst, slot):
        pltpu.make_async_remote_copy(
            src_ref=dst,
            dst_ref=dst,
            send_sem=send_sem.at[slot],
            recv_sem=recv_sem.at[slot],
            device_id=sibling,
            device_id_type=MESH,
        ).wait_recv()

    table_copy = pltpu.make_async_copy(table_ref, table, local_sem.at[4])
    table_copy.start()
    loads = []
    for part in range(4):
        rows = pl.ds(part * 128, 128)
        loads.append(
            (
                pltpu.make_async_copy(momentum_ref.at[rows], moment.at[rows], load_sem.at[part]),
                pltpu.make_async_copy(gradient_ref.at[rows], slope.at[rows], load_sem.at[4 + part]),
            )
        )
        for copy in loads[-1]:
            copy.start()
    g = lax.rem(x, 2) * 4 + y
    weight_copy = pltpu.make_async_copy(
        weight_ref.at[pl.ds(pl.multiple_of(g * BLOCK, BLOCK), BLOCK), pl.ds(pl.multiple_of(c * 512, 512), 512)],
        weight_mine,
        local_sem.at[1],
    )
    weight_copy.start()
    tokens_copy = pltpu.make_async_copy(tokens_ref, tokens_all.at[c], local_sem.at[2])
    tokens_copy.start()

    places = jnp.transpose(indices_ref[...].reshape(128, K).astype(F32)).astype(jnp.int32)
    lane_of = lax.broadcasted_iota(jnp.int32, (128, 128), 1)
    same = (
        lax.broadcasted_iota(jnp.int32, (128, QUAD), 0) // K == lax.broadcasted_iota(jnp.int32, (128, QUAD), 1) // BLOCK
    )
    table_copy.wait()
    all_picks = jnp.zeros((128, 128), F32)
    all_places = jnp.zeros((128, 128), jnp.int32)
    for gx in range(8):
        if gx % 2 == 0:
            for copy in loads[gx // 2]:
                copy.wait()
        for quad in range(4):
            unit = gx * 4 + quad
            rows, columns = pl.ds(gx * BLOCK, BLOCK), pl.ds(quad * QUAD, QUAD)
            place = jnp.concatenate(
                [jnp.broadcast_to(places[:, unit * 4 + i : unit * 4 + i + 1], (K, 128)) for i in range(4)], axis=0
            )
            target = jnp.where(lane_of < BLOCK, place // BLOCK, place % BLOCK + BLOCK)
            hot = jnp.where(target == lane_of, 1.0, 0.0).astype(BF16)
            chosen = jnp.dot(hot, table[:128], preferred_element_type=F32)
            waves[unit] = chosen.astype(BF16)
            moved = momentum_decay * moment[rows, columns] + slope[rows, columns].astype(F32)
            high, low = split(moved)
            partial = jnp.dot(
                chosen[:, :192].astype(BF16), jnp.concatenate([high, low, high], axis=0), preferred_element_type=F32
            )
            terms = jnp.where(same, partial * (chosen[:, 256:512] + chosen[:, 512:]), 0.0)
            picked = jnp.broadcast_to(jnp.sum(terms[:, :128] + terms[:, 128:], axis=1, keepdims=True), (128, 128))
            picks[unit] = picked[:, :BLOCK]
            all_picks = jnp.where(lane_of == unit, picked, all_picks)
            all_places = jnp.where(lane_of == unit, place, all_places)
    all_picks = jnp.transpose(all_picks)
    all_places = jnp.transpose(all_places.astype(F32))
    for unit in range(32):
        packed[unit // 2, unit % 2 : unit % 2 + 1] = all_picks[unit : unit + 1]
        packed[unit // 2, 2 + unit % 2 : 3 + unit % 2] = all_places[unit : unit + 1]

    pl.semaphore_wait(barrier, len(others))
    group_slots = [lane() for _ in group]
    for (d, peer), slot in zip(group, group_slots):
        send(packed.at[peer[0]], got.at[r], slot, peer)
    own_copy = pltpu.make_async_copy(packed.at[r], got.at[r], local_sem.at[0])
    own_copy.start()
    token_slot = lane()
    send(tokens_ref, tokens_all.at[c], token_slot, sibling)

    def leave(gx, carry):
        rows = pl.ds(pl.multiple_of(gx * BLOCK, BLOCK), BLOCK)
        for quad in range(4):
            unit, columns = gx * 4 + quad, pl.ds(quad * QUAD, QUAD)
            wave = waves[unit]
            row_wave = wave[:, :BLOCK].astype(F32) + wave[:, 128:192].astype(F32)
            high, low = split(row_wave * picks[unit])
            zero = jnp.zeros((), BF16)
            col_high, col_low = jnp.where(same, wave[:, 256:512], zero), jnp.where(same, wave[:, 512:], zero)
            back = dot_tn(
                jnp.concatenate([high, high, low], axis=0), jnp.concatenate([col_high, col_low, col_high], axis=0)
            )
            moved = momentum_decay * moment[rows, columns] + slope[rows, columns].astype(F32)
            moment[rows, columns] = moved - back
        pltpu.make_async_copy(moment.at[rows], moment_ref.at[rows], local_sem.at[3]).start()
        return carry

    lax.fori_loop(0, 4, leave, 0)

    own_copy.wait()
    weight_copy.wait()
    for (d, peer), slot in zip(group, group_slots):
        receive(got.at[around(r, -d, 16)], slot)

    freq = lax.broadcasted_iota(jnp.int32, (BLOCK, 128), 0)
    wide = lax.broadcasted_iota(jnp.int32, (QUAD, 128), 0)
    quarter = lax.broadcasted_iota(jnp.int32, (BLOCK, QUAD), 1) // BLOCK
    offset = (lax.broadcasted_iota(jnp.int32, (1, 128), 1) // K) * BLOCK
    fresh = []
    zero = jnp.zeros((), BF16)
    across_high = jnp.concatenate([jnp.where(quarter == i, table[64:128, 256:512], zero) for i in range(4)], axis=0)
    across_low = jnp.concatenate([jnp.where(quarter == i, table[64:128, 512:], zero) for i in range(4)], axis=0)
    across = jnp.concatenate([across_high, across_low, across_high], axis=0)
    for unit in range(2):
        high, low, hot = [], [], []
        for source in range(16):
            value = got[source, unit : unit + 1, :]
            place = got[source, 2 + unit : 3 + unit, :].astype(jnp.int32)
            here = freq == place // BLOCK
            value_high, value_low = split(value)
            high.append(jnp.where(here, value_high.astype(F32), 0.0).astype(BF16))
            low.append(jnp.where(here, value_low.astype(F32), 0.0).astype(BF16))
            hot.append(jnp.where(wide == place % BLOCK + offset, 1.0, 0.0).astype(BF16))
        left = jnp.concatenate([jnp.concatenate(high, axis=1), jnp.concatenate(low, axis=1)], axis=0)
        both = dot_nt(left, jnp.concatenate(hot, axis=1))
        total = both[:BLOCK] + both[BLOCK:]
        high, low = split(total)
        inner = jnp.dot(
            table[128:, :192], jnp.concatenate([high, low, high], axis=0), preferred_element_type=F32
        )
        high, low = split(inner)
        update = jnp.dot(jnp.concatenate([high, high, low], axis=1), across, preferred_element_type=F32) / 16.0
        old = weight_mine[:, unit * QUAD : (unit + 1) * QUAD].astype(F32)
        fresh.append((old - step_size * update).astype(BF16))
    big[q, p, z] = fresh[0]
    mid[p, q, z] = fresh[1][:, :128]
    small[z, q, p] = fresh[1][:, 128:]

    p_next, p_last = p_peers[0][1], p_peers[2][1]
    q_next, q_last = q_peers[0][1], q_peers[2][1]
    z_next, z_last = z_peers[0][1], z_peers[6][1]
    small_1 = [lane() for _ in p_peers]
    mid_1 = [lane() for _ in z_peers]
    big_1 = [lane() for _ in z_peers]
    small_2 = [lane() for _ in q_peers]
    mid_2 = [lane() for _ in q_peers]
    big_2 = [lane() for _ in p_peers]
    mid_3 = [(lane(), lane()) for _ in range(4)]
    big_3 = [(lane(), lane()) for _ in range(4)]
    mid_4 = [lane() for _ in range(4)]
    big_4 = [lane() for _ in range(4)]
    small_3 = [[(lane(), lane()) for _ in range(2)] for _ in range(4)]
    near_first = [z_peers[d - 1] for d in (1, 7, 2, 6, 3, 5, 4)]

    mid_line = [(mid_3[0][0], p_next), (mid_3[0][1], p_last)] + [(mid_2[d - 1], q_peers[d - 1][1]) for d in (1, 3, 2)]
    big_line = [(big_3[0][0], q_next), (big_3[0][1], q_last)] + [(big_2[d - 1], p_peers[d - 1][1]) for d in (1, 3, 2)]
    for buffer, first, second, line in ((mid, p, q, mid_line), (big, q, p, big_line)):
        for slot, peer in line:
            whole.append((buffer.at[first, second], slot))

    def along(buffer, first, second, place, line):
        here = buffer.at[first, second, place]
        for slot, peer in line:
            send(here, here, slot, peer, keep=False)

    for (d, peer), slot in zip(p_peers, small_1):
        send(small.at[z, q, p], small.at[z, q, p], slot, peer)
    for d, peer in near_first:
        send(mid.at[p, q, z], mid.at[p, q, z], mid_1[d - 1], peer)
        send(big.at[q, p, z], big.at[q, p, z], big_1[d - 1], peer)
    along(mid, p, q, z, mid_line)
    along(big, q, p, z, big_line)

    lax.fori_loop(4, 8, leave, 0)

    for (d, peer), slot in zip(p_peers, small_1):
        receive(small.at[z, q, around(p, -d, 4)], slot)
    for (d, peer), slot in zip(q_peers, small_2):
        send(small.at[z, q], small.at[z, q], slot, peer)

    halves = [pl.ds(0, 2), pl.ds(2, 2)]
    for turn, (d, _) in enumerate(near_first):
        place = around(z, -d, 8)
        receive(mid.at[p, q, place], mid_1[d - 1])
        along(mid, p, q, place, mid_line)
        receive(big.at[q, p, place], big_1[d - 1])
        along(big, q, p, place, big_line)
        if turn == 3:
            for (d, peer), slot in zip(q_peers, small_2):
                receive(small.at[z, around(q, -d, 4)], slot)
            for half in range(2):
                send(small.at[z, halves[half]], small.at[z, halves[half]], small_3[0][half][0], z_next)
                send(small.at[z, halves[half]], small.at[z, halves[half]], small_3[0][half][1], z_last)

    for d in (1, 3, 2):
        here = mid.at[p, around(q, -d, 4)]
        receive(here, mid_2[d - 1])
        send(here, here, mid_3[d][0], p_next)
        send(here, here, mid_3[d][1], p_last)
        here = big.at[q, around(p, -d, 4)]
        receive(here, big_2[d - 1])
        send(here, here, big_3[d][0], q_next)
        send(here, here, big_3[d][1], q_last)

    def small_step(step):
        before, after = around(z, -step, 8), around(z, step, 8)
        for half in range(2):
            receive(small.at[before, halves[half]], small_3[step - 1][half][0])
            if step < 3 or half == 0:
                here = small.at[before, halves[half]]
                send(here, here, small_3[step][half][0], z_next)
            receive(small.at[after, halves[half]], small_3[step - 1][half][1])
            if step < 3 or half == 1:
                here = small.at[after, halves[half]]
                send(here, here, small_3[step][half][1], z_last)

    for turn, d in enumerate((0, 1, 3, 2)):
        for buffer, slots, onward, first, second, ahead, behind in (
            (mid, mid_3, mid_4, p, q, p_next, p_last),
            (big, big_3, big_4, q, p, q_next, q_last),
        ):
            sub = around(second, -d, 4)
            left = buffer.at[around(first, -1, 4), sub]
            right = buffer.at[around(first, 1, 4), sub]
            receive(left, slots[d][0])
            if d in (0, 2):
                send(left, left, onward[d], ahead)
            receive(right, slots[d][1])
            if d in (1, 3):
                send(right, right, onward[d], behind)
        if turn < 3:
            small_step(turn + 1)

    opposite = around(z, 4, 8)
    for d in (0, 1, 3, 2):
        receive(mid.at[around(p, 2, 4), around(q, -d, 4)], mid_4[d])
        receive(big.at[around(q, 2, 4), around(p, -d, 4)], big_4[d])
    receive(small.at[opposite, halves[0]], small_3[3][0][0])
    receive(small.at[opposite, halves[1]], small_3[3][1][1])

    weight_slot = lane()
    keys_slot = lane()

    def rows_of(zi, xi, yi):
        pi, qi = xi + c * (yi - xi), yi + c * (xi - yi)
        return jnp.concatenate([big[qi, pi, zi], mid[pi, qi, zi], small[zi, qi, pi]], axis=1)

    x_high = 2 * lax.rem(f, 2)
    for xi in range(2):
        for yi in range(4):
            fresh_ref[c, xi * 4 + yi] = rows_of(z, x_high + xi, yi)
    send(fresh_ref.at[c], fresh_ref.at[c], weight_slot, sibling)

    tokens_copy.wait()
    receive(tokens_all.at[1 - c], token_slot)
    total_acc[...] = jnp.zeros_like(total_acc)

    def multiply(zi, carry):
        right = jnp.concatenate([rows_of(zi, xi, yi) for xi in range(4) for yi in range(4)], axis=0)
        depth = pl.ds(pl.multiple_of(zi * 1024, 1024), 1024)
        for half in range(2):
            total_acc[half] += jnp.dot(tokens_all[half, :, depth], right, preferred_element_type=F32)
        return carry

    lax.fori_loop(0, 8, multiply, 0)
    keys_ref[c] = total_acc[c].astype(BF16)
    got_keys = total_acc[1 - c].astype(BF16)
    tokens_all[0, :, :512] = got_keys
    send(tokens_all.at[0, :, pl.ds(0, 512)], keys_ref.at[c], keys_slot, sibling)
    receive(fresh_ref.at[1 - c], weight_slot)
    receive(keys_ref.at[1 - c], keys_slot)
    pltpu.make_async_copy(moment, moment_ref, local_sem.at[3]).wait()
    for copy in started:
        copy.wait_send()
    for line, slot in whole:
        pltpu.make_async_remote_copy(
            src_ref=line,
            dst_ref=line,
            send_sem=send_sem.at[slot],
            recv_sem=recv_sem.at[slot],
            device_id=sibling,
            device_id_type=MESH,
        ).wait_send()


def step(table, indices, momentum, gradient, weight, tokens):
    vmem = pl.BlockSpec(memory_space=pltpu.VMEM)
    hbm = pl.BlockSpec(memory_space=pl.ANY)
    slots = 128
    return pl.pallas_call(
        step_kernel,
        in_specs=[hbm, vmem, hbm, hbm, hbm, hbm],
        out_specs=[vmem, vmem, hbm],
        out_shape=[
            jax.ShapeDtypeStruct((2, 256, 512), BF16),
            jax.ShapeDtypeStruct((2, 8, 64, 512), BF16),
            jax.ShapeDtypeStruct((512, 1024), F32),
        ],
        scratch_shapes=[
            pltpu.VMEM((192, 768), BF16),
            pltpu.VMEM((512, 1024), F32),
            pltpu.VMEM((512, 1024), BF16),
            pltpu.VMEM((32, 128, 768), BF16),
            pltpu.VMEM((32, 128, 64), F32),
            pltpu.VMEM((16, 8, 128), F32),
            pltpu.VMEM((2, 256, 8192), BF16),
            pltpu.VMEM((64, 512), BF16),
            pltpu.VMEM((16, 8, 128), F32),
            pltpu.VMEM((4, 4, 8, 64, 256), BF16),
            pltpu.VMEM((4, 4, 8, 64, 128), BF16),
            pltpu.VMEM((8, 4, 4, 64, 128), BF16),
            pltpu.VMEM((2, 256, 512), F32),
            pltpu.SemaphoreType.DMA((5,)),
            pltpu.SemaphoreType.DMA((8,)),
            pltpu.SemaphoreType.DMA((slots,)),
            pltpu.SemaphoreType.DMA((slots,)),
        ],
        compiler_params=pltpu.CompilerParams(collective_id=0, has_side_effects=True, vmem_limit_bytes=60 * 2**20),
    )(table, indices, momentum, gradient, weight, tokens)


def per_device(tokens, weight, momentum, gradient, indices):
    keys, fresh, moment = step(jnp.asarray(tables()), indices[0], momentum[0], gradient[0], weight, tokens)
    keys = jnp.concatenate([keys[0], keys[1]], axis=1)
    fresh = fresh.reshape(2, 512, 512)
    fresh = jnp.concatenate([fresh[0], fresh[1]], axis=1)
    return (keys, fresh, moment[None])


def solution(mesh):
    return jax.shard_map(
        per_device,
        mesh=mesh,
        in_specs=(
            P(("replica", "fsdp"), None),
            P("fsdp", None),
            P("replica", "fsdp", None),
            P("replica", "fsdp", None),
            P("replica", "fsdp", None, None),
        ),
        out_specs=(P(("replica", "fsdp"), None), P("fsdp", None), P("replica", "fsdp", None)),
        check_vma=False,
    )
```

```python
import functools

import jax
import jax.numpy as jnp
import ml_dtypes
import numpy as np
from jax import lax
from jax.experimental import pallas as pl
from jax.experimental.pallas import tpu as pltpu
from jax.sharding import PartitionSpec as P

BLOCK = 64
K = 32
QUAD = 256
MESH = pl.DeviceIdType.MESH
F32 = jnp.float32
BF16 = jnp.bfloat16

momentum_decay = 0.9
step_size = 0.1


def dct_table(size):
    freq = np.arange(size, dtype=np.float64)[:, None]
    place = np.arange(size, dtype=np.float64)[None, :]
    scale = np.where(freq == 0, np.sqrt(1.0 / size), np.sqrt(2.0 / size))
    return (scale * np.cos(np.pi * (2.0 * place + 1.0) * freq / (2.0 * size))).astype(np.float32)


def tables():
    table = dct_table(BLOCK)
    high = table.astype(ml_dtypes.bfloat16)
    low = (table - high.astype(np.float32)).astype(ml_dtypes.bfloat16)
    out = np.zeros((192, 512), ml_dtypes.bfloat16)
    out[:64, :192] = np.concatenate([high, high, low], axis=1)
    out[64:128, 256:384] = np.tile(high, (1, 2))
    out[64:128, 384:512] = np.tile(low, (1, 2))
    out[128:, :192] = np.concatenate([high.T, high.T, low.T], axis=1)
    return out


def split(value):
    high = value.astype(BF16)
    return high, (value - high.astype(F32)).astype(BF16)


def dot_tn(a, b):
    return lax.dot_general(a, b, (((0,), (0,)), ((), ())), preferred_element_type=F32)


def dot_nt(a, b):
    return lax.dot_general(a, b, (((1,), (1,)), ((), ())), preferred_element_type=F32)


def step_kernel(
    table_ref,
    indices_ref,
    momentum_ref,
    gradient_ref,
    weight_ref,
    tokens_ref,
    keys_ref,
    fresh_ref,
    moment_ref,
    table,
    moment,
    slope,
    waves,
    picks,
    packed,
    tokens_all,
    weight_mine,
    got,
    big,
    mid,
    small,
    total_acc,
    far_tokens,
    theirs,
    ours,
    block,
    local_sem,
    load_sem,
    send_sem,
    recv_sem,
):
    r, f = lax.axis_index("replica"), lax.axis_index("fsdp")
    x = lax.rem(f, 2) * 2 + r // 8
    y = lax.rem(r // 2, 4)
    z = f // 2
    c = lax.rem(r, 2)
    p, q = x + c * (y - x), y + c * (x - y)

    def device(p, q, z, c=c):
        x, y = p + c * (q - p), q + c * (p - q)
        return (lax.rem(x, 2) * 8 + y * 2 + c, z * 2 + x // 2)

    def around(value, step, size):
        return lax.rem(value + step + size, size)

    sibling = (r + 1 - 2 * c, f)
    z_peers = [(d, device(p, q, around(z, d, 8))) for d in range(1, 8)]
    p_peers = [(d, device(around(p, d, 4), q, z)) for d in range(1, 4)]
    q_peers = [(d, device(p, around(q, d, 4), z)) for d in range(1, 4)]
    group = [(d, (lax.rem(r + d, 16), f)) for d in range(1, 16)]
    x_far = [(lax.rem(r + d, 16), f + 1 - 2 * lax.rem(f, 2)) for d in (0, 8)]

    barrier = pltpu.get_barrier_semaphore()
    others = [peer for _, peer in z_peers + group] + x_far
    for peer in others:
        pl.semaphore_signal(barrier, inc=1, device_id=peer, device_id_type=MESH)

    started, whole = [], []
    count = [0]

    def lane():
        count[0] += 1
        return count[0] - 1

    def send(src, dst, slot, peer, keep=True):
        copy = pltpu.make_async_remote_copy(
            src_ref=src,
            dst_ref=dst,
            send_sem=send_sem.at[slot],
            recv_sem=recv_sem.at[slot],
            device_id=peer,
            device_id_type=MESH,
        )
        copy.start()
        if keep:
            started.append(copy)

    def receive(dst, slot):
        pltpu.make_async_remote_copy(
            src_ref=dst,
            dst_ref=dst,
            send_sem=send_sem.at[slot],
            recv_sem=recv_sem.at[slot],
            device_id=sibling,
            device_id_type=MESH,
        ).wait_recv()

    table_copy = pltpu.make_async_copy(table_ref, table, local_sem.at[4])
    table_copy.start()
    loads = []
    for part in range(4):
        rows = pl.ds(part * 128, 128)
        loads.append(
            (
                pltpu.make_async_copy(momentum_ref.at[rows], moment.at[rows], load_sem.at[part]),
                pltpu.make_async_copy(gradient_ref.at[rows], slope.at[rows], load_sem.at[4 + part]),
            )
        )
        for copy in loads[-1]:
            copy.start()
    g = lax.rem(x, 2) * 4 + y
    weight_copy = pltpu.make_async_copy(
        weight_ref.at[pl.ds(pl.multiple_of(g * BLOCK, BLOCK), BLOCK), pl.ds(pl.multiple_of(c * 512, 512), 512)],
        weight_mine,
        local_sem.at[1],
    )
    weight_copy.start()
    tokens_copy = pltpu.make_async_copy(tokens_ref, tokens_all.at[c], local_sem.at[2])
    tokens_copy.start()

    places = jnp.transpose(indices_ref[...].reshape(128, K).astype(F32)).astype(jnp.int32)
    lane_of = lax.broadcasted_iota(jnp.int32, (128, 128), 1)
    same = ((lax.broadcasted_iota(jnp.int32, (128, 128), 0) >> 5) & 1) == (lane_of >> 6)
    table_copy.wait()
    all_picks = jnp.zeros((128, 128), F32)
    all_places = jnp.zeros((128, 128), jnp.int32)
    for gx in range(8):
        if gx % 2 == 0:
            for copy in loads[gx // 2]:
                copy.wait()
        for quad in range(4):
            unit = gx * 4 + quad
            rows, columns = pl.ds(gx * BLOCK, BLOCK), pl.ds(quad * QUAD, QUAD)
            place = jnp.concatenate(
                [jnp.broadcast_to(places[:, unit * 4 + i : unit * 4 + i + 1], (K, 128)) for i in range(4)], axis=0
            )
            target = jnp.where(lane_of < BLOCK, place >> 6, (place & 63) + BLOCK)
            hot = jnp.where(target == lane_of, 1.0, 0.0).astype(BF16)
            chosen = jnp.dot(hot, table[:128], preferred_element_type=F32)
            waves[unit] = chosen.astype(BF16)
            moved = momentum_decay * moment[rows, columns] + slope[rows, columns].astype(F32)
            high, low = split(moved)
            three = jnp.concatenate([high, low, high], axis=0)
            chosen_row = chosen[:, :192].astype(BF16)
            partial = jnp.concatenate(
                [
                    jnp.dot(chosen_row[:BLOCK], three[:, :128], preferred_element_type=F32),
                    jnp.dot(chosen_row[BLOCK:], three[:, 128:], preferred_element_type=F32),
                ],
                axis=0,
            )
            terms = jnp.where(same, partial * (chosen[:, 256:384] + chosen[:, 384:]), 0.0)
            picked = jnp.broadcast_to(jnp.sum(terms, axis=1, keepdims=True), (128, 128))
            picks[unit] = picked[:, :BLOCK]
            all_picks = jnp.where(lane_of == unit, picked, all_picks)
            all_places = jnp.where(lane_of == unit, place, all_places)
    all_picks = jnp.transpose(all_picks)
    all_places = jnp.transpose(all_places.astype(F32))
    for unit in range(32):
        packed[unit // 2, unit % 2 : unit % 2 + 1] = all_picks[unit : unit + 1]
        packed[unit // 2, 2 + unit % 2 : 3 + unit % 2] = all_places[unit : unit + 1]

    pl.semaphore_wait(barrier, len(others))
    group_slots = [lane() for _ in group]
    for (d, peer), slot in zip(group, group_slots):
        send(packed.at[peer[0]], got.at[r], slot, peer)
    own_copy = pltpu.make_async_copy(packed.at[r], got.at[r], local_sem.at[0])
    own_copy.start()
    token_slot = lane()
    send(tokens_ref, tokens_all.at[c], token_slot, sibling)

    def leave(gx, carry):
        rows = pl.ds(pl.multiple_of(gx * BLOCK, BLOCK), BLOCK)
        for quad in range(4):
            unit, columns = gx * 4 + quad, pl.ds(quad * QUAD, QUAD)
            wave = waves[unit]
            row_wave = wave[:, :BLOCK].astype(F32) + wave[:, 128:192].astype(F32)
            high, low = split(row_wave * picks[unit])
            zero = jnp.zeros((), BF16)
            col_high, col_low = jnp.where(same, wave[:, 256:384], zero), jnp.where(same, wave[:, 384:], zero)
            back = []
            for pair in (slice(0, BLOCK), slice(BLOCK, 128)):
                back.append(
                    dot_tn(
                        jnp.concatenate([high[pair], high[pair], low[pair]], axis=0),
                        jnp.concatenate([col_high[pair], col_low[pair], col_high[pair]], axis=0),
                    )
                )
            back = jnp.concatenate(back, axis=1)
            moved = momentum_decay * moment[rows, columns] + slope[rows, columns].astype(F32)
            moment[rows, columns] = moved - back
        pltpu.make_async_copy(moment.at[rows], moment_ref.at[rows], local_sem.at[3]).start()
        return carry

    lax.fori_loop(0, 4, leave, 0)

    own_copy.wait()
    weight_copy.wait()
    for (d, peer), slot in zip(group, group_slots):
        receive(got.at[around(r, -d, 16)], slot)

    freq = lax.broadcasted_iota(jnp.int32, (BLOCK, 128), 0)
    wide = lax.broadcasted_iota(jnp.int32, (QUAD, 128), 0)
    quarter = lax.broadcasted_iota(jnp.int32, (BLOCK, QUAD), 1) // BLOCK
    offset = (lax.broadcasted_iota(jnp.int32, (1, 128), 1) // K) * BLOCK
    fresh = []
    zero = jnp.zeros((), BF16)
    tile_high = jnp.concatenate([table[64:128, 256:384]] * 2, axis=1)
    tile_low = jnp.concatenate([table[64:128, 384:]] * 2, axis=1)
    across_high = jnp.concatenate([jnp.where(quarter == i, tile_high, zero) for i in range(4)], axis=0)
    across_low = jnp.concatenate([jnp.where(quarter == i, tile_low, zero) for i in range(4)], axis=0)
    across = jnp.concatenate([across_high, across_low, across_high], axis=0)
    for unit in range(2):
        high, low, hot = [], [], []
        for source in range(16):
            value = got[source, unit : unit + 1, :]
            place = got[source, 2 + unit : 3 + unit, :].astype(jnp.int32)
            here = freq == place >> 6
            value_high, value_low = split(value)
            high.append(jnp.where(here, value_high.astype(F32), 0.0).astype(BF16))
            low.append(jnp.where(here, value_low.astype(F32), 0.0).astype(BF16))
            hot.append(jnp.where(wide == (place & 63) + offset, 1.0, 0.0).astype(BF16))
        left = jnp.concatenate([jnp.concatenate(high, axis=1), jnp.concatenate(low, axis=1)], axis=0)
        both = dot_nt(left, jnp.concatenate(hot, axis=1))
        total = both[:BLOCK] + both[BLOCK:]
        high, low = split(total)
        inner = jnp.dot(
            table[128:, :192], jnp.concatenate([high, low, high], axis=0), preferred_element_type=F32
        )
        high, low = split(inner)
        update = jnp.dot(jnp.concatenate([high, high, low], axis=1), across, preferred_element_type=F32) / 16.0
        old = weight_mine[:, unit * QUAD : (unit + 1) * QUAD].astype(F32)
        fresh.append((old - step_size * update).astype(BF16))
    big[q, p, z] = fresh[0]
    mid[p, q, z] = fresh[1][:, :128]
    small[z, q, p] = fresh[1][:, 128:]

    p_next, p_last = p_peers[0][1], p_peers[2][1]
    q_next, q_last = q_peers[0][1], q_peers[2][1]
    z_next, z_last = z_peers[0][1], z_peers[6][1]
    small_1 = [lane() for _ in p_peers]
    mid_1 = [lane() for _ in z_peers]
    big_1 = [lane() for _ in z_peers]
    small_2 = [lane() for _ in q_peers]
    mid_2 = [lane() for _ in q_peers]
    big_2 = [lane() for _ in p_peers]
    mid_3 = [(lane(), lane()) for _ in range(4)]
    big_3 = [(lane(), lane()) for _ in range(4)]
    mid_4 = [lane() for _ in range(4)]
    big_4 = [lane() for _ in range(4)]
    small_3 = [[(lane(), lane()) for _ in range(2)] for _ in range(4)]
    near_first = [z_peers[d - 1] for d in (1, 7, 2, 6, 3, 5, 4)]

    mid_line = [(mid_3[0][0], p_next), (mid_3[0][1], p_last)] + [(mid_2[d - 1], q_peers[d - 1][1]) for d in (1, 3, 2)]
    big_line = [(big_3[0][0], q_next), (big_3[0][1], q_last)] + [(big_2[d - 1], p_peers[d - 1][1]) for d in (1, 3, 2)]
    for buffer, first, second, line in ((mid, p, q, mid_line), (big, q, p, big_line)):
        for slot, peer in line:
            whole.append((buffer.at[first, second], slot))

    def along(buffer, first, second, place, line):
        here = buffer.at[first, second, place]
        for slot, peer in line:
            send(here, here, slot, peer, keep=False)

    for (d, peer), slot in zip(p_peers, small_1):
        send(small.at[z, q, p], small.at[z, q, p], slot, peer)
    for d, peer in near_first:
        send(mid.at[p, q, z], mid.at[p, q, z], mid_1[d - 1], peer)
        send(big.at[q, p, z], big.at[q, p, z], big_1[d - 1], peer)
    along(mid, p, q, z, mid_line)
    along(big, q, p, z, big_line)

    lax.fori_loop(4, 8, leave, 0)

    for (d, peer), slot in zip(p_peers, small_1):
        receive(small.at[z, q, around(p, -d, 4)], slot)
    for (d, peer), slot in zip(q_peers, small_2):
        send(small.at[z, q], small.at[z, q], slot, peer)

    halves = [pl.ds(0, 2), pl.ds(2, 2)]
    for turn, (d, _) in enumerate(near_first):
        place = around(z, -d, 8)
        receive(mid.at[p, q, place], mid_1[d - 1])
        along(mid, p, q, place, mid_line)
        receive(big.at[q, p, place], big_1[d - 1])
        along(big, q, p, place, big_line)
        if turn == 3:
            for (d, peer), slot in zip(q_peers, small_2):
                receive(small.at[z, around(q, -d, 4)], slot)
            for half in range(2):
                send(small.at[z, halves[half]], small.at[z, halves[half]], small_3[0][half][0], z_next)
                send(small.at[z, halves[half]], small.at[z, halves[half]], small_3[0][half][1], z_last)

    p_far, q_far = around(p, 2, 4), around(q, 2, 4)
    tokens_copy.wait()
    receive(tokens_all.at[1 - c], token_slot)

    def piece(half, xi, yi, zi):
        start = pl.multiple_of(zi * 1024 + xi * 256 + (yi // 2) * 128, 128)
        return tokens_all[half, :, pl.ds(start, 128)]

    def line_up(i, carry):
        line, zi = i // 4, lax.rem(i, 4) * 2
        spot = pl.ds(pl.multiple_of(i * 128, 128), 128)
        for which, (pi, qi) in enumerate(((line, q_far), (p_far, line))):
            xi, yi = pi + c * (qi - pi), qi + c * (pi - qi)
            odd = lax.rem(yi, 2)

            def take(low):
                for half in range(2):
                    one, two = piece(half, xi, yi, zi), piece(half, xi, yi, zi + 1)
                    far_tokens[which, half, :, spot] = jnp.concatenate(
                        [one[:, low : low + BLOCK], two[:, low : low + BLOCK]], axis=1
                    )

            pl.when(odd == 0)(functools.partial(take, 0))
            pl.when(odd == 1)(functools.partial(take, BLOCK))
        return carry

    def small_step(step):
        before, after = around(z, -step, 8), around(z, step, 8)
        for half in range(2):
            receive(small.at[before, halves[half]], small_3[step - 1][half][0])
            if step < 3 or half == 0:
                here = small.at[before, halves[half]]
                send(here, here, small_3[step][half][0], z_next)
            receive(small.at[after, halves[half]], small_3[step - 1][half][1])
            if step < 3 or half == 1:
                here = small.at[after, halves[half]]
                send(here, here, small_3[step][half][1], z_last)

    for turn, d in enumerate((1, 3, 2)):
        here = mid.at[p, around(q, -d, 4)]
        receive(here, mid_2[d - 1])
        send(here, here, mid_3[d][0], p_next)
        send(here, here, mid_3[d][1], p_last)
        here = big.at[q, around(p, -d, 4)]
        receive(here, big_2[d - 1])
        send(here, here, big_3[d][0], q_next)
        send(here, here, big_3[d][1], q_last)
        if turn == 1:
            small_step(1)

    small_step(2)
    for turn, d in enumerate((0, 1, 3, 2)):
        for buffer, slots, onward, first, second, ahead, behind in (
            (mid, mid_3, mid_4, p, q, p_next, p_last),
            (big, big_3, big_4, q, p, q_next, q_last),
        ):
            sub = around(second, -d, 4)
            left = buffer.at[around(first, -1, 4), sub]
            right = buffer.at[around(first, 1, 4), sub]
            receive(left, slots[d][0])
            if d in (0, 2):
                send(left, left, onward[d], ahead)
            receive(right, slots[d][1])
            if d in (1, 3):
                send(right, right, onward[d], behind)
        if turn == 2:
            small_step(3)
        if turn < 3:
            lax.fori_loop((0, 6, 11)[turn], (6, 11, 16)[turn], line_up, 0)

    opposite = around(z, 4, 8)
    total_acc[...] = jnp.zeros_like(total_acc)

    def known_rows(zi, xi, yi):
        pi, qi = xi + c * (yi - xi), yi + c * (xi - yi)
        none = jnp.zeros((), BF16)
        pw = pi + (p - pi) * (pi == p_far).astype(jnp.int32)
        qw = qi + (q - qi) * (qi == q_far).astype(jnp.int32)
        zw = zi + (z - zi) * (zi == opposite).astype(jnp.int32)
        return jnp.concatenate(
            [
                jnp.where(qi == q_far, none, big[qw, pi, zi]),
                jnp.where(pi == p_far, none, mid[pw, qi, zi]),
                jnp.where(zi == opposite, none, small[zw, qi, pi]),
            ],
            axis=1,
        )

    def multiply(zi, carry):
        right = jnp.concatenate([known_rows(zi, xi, yi) for xi in range(4) for yi in range(4)], axis=0)
        depth = pl.ds(pl.multiple_of(zi * 1024, 1024), 1024)
        for half in range(2):
            total_acc[half] += jnp.dot(tokens_all[half, :, depth], right, preferred_element_type=F32)
        return carry

    lax.fori_loop(0, 8, multiply, 0)

    for d in (0, 1, 3, 2):
        receive(mid.at[around(p, 2, 4), around(q, -d, 4)], mid_4[d])
        receive(big.at[around(q, 2, 4), around(p, -d, 4)], big_4[d])
    receive(small.at[opposite, halves[0]], small_3[3][0][0])
    receive(small.at[opposite, halves[1]], small_3[3][1][1])

    weight_slot = lane()
    keys_slot = lane()

    def rows_of(zi, xi, yi):
        pi, qi = xi + c * (yi - xi), yi + c * (xi - yi)
        return jnp.concatenate([big[qi, pi, zi], mid[pi, qi, zi], small[zi, qi, pi]], axis=1)

    x_high = 2 * lax.rem(f, 2)
    for xi in range(2):
        for yi in range(4):
            block[xi * 4 + yi] = rows_of(z, x_high + xi, yi)
    send(block, fresh_ref.at[c], weight_slot, sibling)
    block_copy = pltpu.make_async_copy(block, fresh_ref.at[c], local_sem.at[0])
    block_copy.start()

    far_small = jnp.concatenate(
        [
            small[opposite, yi + c * (xi - yi), xi + c * (yi - xi)]
            for xi in range(4)
            for yi in range(4)
        ],
        axis=0,
    )
    depth = pl.ds(pl.multiple_of(opposite * 1024, 1024), 1024)

    def finish(half):
        sums = jnp.concatenate(
            [
                jnp.dot(far_tokens[0, half], big[q_far].reshape(2048, 256), preferred_element_type=F32),
                jnp.dot(far_tokens[1, half], mid[p_far].reshape(2048, 128), preferred_element_type=F32),
                jnp.dot(tokens_all[half, :, depth], far_small, preferred_element_type=F32),
            ],
            axis=1,
        )
        return (total_acc[half] + sums).astype(BF16)

    theirs[...] = finish(1 - c)
    send(theirs, keys_ref.at[c], keys_slot, sibling)
    ours[...] = finish(c)
    keys_copy = pltpu.make_async_copy(ours, keys_ref.at[c], local_sem.at[1])
    keys_copy.start()
    block_copy.wait()
    keys_copy.wait()
    receive(fresh_ref.at[1 - c], weight_slot)
    receive(keys_ref.at[1 - c], keys_slot)
    pltpu.make_async_copy(moment, moment_ref, local_sem.at[3]).wait()
    for copy in started:
        copy.wait_send()
    for line, slot in whole:
        pltpu.make_async_remote_copy(
            src_ref=line,
            dst_ref=line,
            send_sem=send_sem.at[slot],
            recv_sem=recv_sem.at[slot],
            device_id=sibling,
            device_id_type=MESH,
        ).wait_send()


def step(table, indices, momentum, gradient, weight, tokens):
    vmem = pl.BlockSpec(memory_space=pltpu.VMEM)
    hbm = pl.BlockSpec(memory_space=pl.ANY)
    slots = 128
    return pl.pallas_call(
        step_kernel,
        in_specs=[hbm, vmem, hbm, hbm, hbm, hbm],
        out_specs=[hbm, hbm, hbm],
        out_shape=[
            jax.ShapeDtypeStruct((2, 256, 512), BF16),
            jax.ShapeDtypeStruct((2, 8, 64, 512), BF16),
            jax.ShapeDtypeStruct((512, 1024), F32),
        ],
        scratch_shapes=[
            pltpu.VMEM((192, 512), BF16),
            pltpu.VMEM((512, 1024), F32),
            pltpu.VMEM((512, 1024), BF16),
            pltpu.VMEM((32, 128, 512), BF16),
            pltpu.VMEM((32, 128, 64), F32),
            pltpu.VMEM((16, 8, 128), F32),
            pltpu.VMEM((2, 256, 8192), BF16),
            pltpu.VMEM((64, 512), BF16),
            pltpu.VMEM((16, 8, 128), F32),
            pltpu.VMEM((4, 4, 8, 64, 256), BF16),
            pltpu.VMEM((4, 4, 8, 64, 128), BF16),
            pltpu.VMEM((8, 4, 4, 64, 128), BF16),
            pltpu.VMEM((2, 256, 512), F32),
            pltpu.VMEM((2, 2, 256, 2048), BF16),
            pltpu.VMEM((256, 512), BF16),
            pltpu.VMEM((256, 512), BF16),
            pltpu.VMEM((8, 64, 512), BF16),
            pltpu.SemaphoreType.DMA((5,)),
            pltpu.SemaphoreType.DMA((8,)),
            pltpu.SemaphoreType.DMA((slots,)),
            pltpu.SemaphoreType.DMA((slots,)),
        ],
        compiler_params=pltpu.CompilerParams(collective_id=0, has_side_effects=True, vmem_limit_bytes=60 * 2**20),
    )(table, indices, momentum, gradient, weight, tokens)


def place_kernel(keys_in, fresh_in, moment_in, keys_out, fresh_out, moment_out, keys, fresh, moment, in_sem, out_sem):
    moves = []
    for half in range(2):
        columns = pl.ds(half * 512, 512)
        for part in range(2):
            rows = pl.ds(part * 128, 128)
            moves.append((keys_in.at[half, rows], keys.at[half, rows], keys_out.at[rows, columns]))
        for part in range(4):
            rows = pl.ds(part * 128, 128)
            moves.append((fresh_in.at[half, rows], fresh.at[half, rows], fresh_out.at[rows, columns]))
    for part in range(8):
        rows = pl.ds(part * 64, 64)
        moves.append((moment_in.at[rows], moment.at[rows], moment_out.at[rows]))
    ins = [pltpu.make_async_copy(a, b, in_sem.at[i]) for i, (a, b, _) in enumerate(moves)]
    outs = [pltpu.make_async_copy(b, o, out_sem.at[i]) for i, (_, b, o) in enumerate(moves)]
    for copy in ins:
        copy.start()
    for copy, onward in zip(ins, outs):
        copy.wait()
        onward.start()
    for copy in outs:
        copy.wait()


def put_in_place(keys, fresh, moment):
    hbm = pl.BlockSpec(memory_space=pl.ANY)
    return pl.pallas_call(
        place_kernel,
        in_specs=[hbm] * 3,
        out_specs=[hbm] * 3,
        out_shape=[
            jax.ShapeDtypeStruct((256, 1024), BF16),
            jax.ShapeDtypeStruct((512, 1024), BF16),
            jax.ShapeDtypeStruct((512, 1024), F32),
        ],
        scratch_shapes=[
            pltpu.VMEM((2, 256, 512), BF16),
            pltpu.VMEM((2, 512, 512), BF16),
            pltpu.VMEM((512, 1024), F32),
            pltpu.SemaphoreType.DMA((20,)),
            pltpu.SemaphoreType.DMA((20,)),
        ],
        compiler_params=pltpu.CompilerParams(vmem_limit_bytes=63 * 2**20),
    )(keys, fresh, moment)


def per_device(tokens, weight, momentum, gradient, indices):
    keys, fresh, moment = step(jnp.asarray(tables()), indices[0], momentum[0], gradient[0], weight, tokens)
    keys, fresh, moment = put_in_place(keys, fresh.reshape(2, 512, 512), moment)
    return (keys, fresh, moment[None])


def solution(mesh):
    return jax.shard_map(
        per_device,
        mesh=mesh,
        in_specs=(
            P(("replica", "fsdp"), None),
            P("fsdp", None),
            P("replica", "fsdp", None),
            P("replica", "fsdp", None),
            P("replica", "fsdp", None, None),
        ),
        out_specs=(P(("replica", "fsdp"), None), P("fsdp", None), P("replica", "fsdp", None)),
        check_vma=False,
    )
```

```python
import functools

import jax
import jax.numpy as jnp
import ml_dtypes
import numpy as np
from jax import lax
from jax.experimental import pallas as pl
from jax.experimental.pallas import tpu as pltpu
from jax.sharding import PartitionSpec as P

BLOCK = 64
K = 32
QUAD = 256
MESH = pl.DeviceIdType.MESH
F32 = jnp.float32
BF16 = jnp.bfloat16

momentum_decay = 0.9
step_size = 0.1


def dct_table(size):
    freq = np.arange(size, dtype=np.float64)[:, None]
    place = np.arange(size, dtype=np.float64)[None, :]
    scale = np.where(freq == 0, np.sqrt(1.0 / size), np.sqrt(2.0 / size))
    return (scale * np.cos(np.pi * (2.0 * place + 1.0) * freq / (2.0 * size))).astype(np.float32)


def tables():
    table = dct_table(BLOCK)
    high = table.astype(ml_dtypes.bfloat16)
    low = (table - high.astype(np.float32)).astype(ml_dtypes.bfloat16)
    out = np.zeros((192, 512), ml_dtypes.bfloat16)
    out[:64, :192] = np.concatenate([high, high, low], axis=1)
    out[64:128, 256:384] = np.tile(high, (1, 2))
    out[64:128, 384:512] = np.tile(low, (1, 2))
    out[128:, :192] = np.concatenate([high.T, high.T, low.T], axis=1)
    return out


def split(value):
    high = value.astype(BF16)
    return high, (value - high.astype(F32)).astype(BF16)


def dot_tn(a, b):
    return lax.dot_general(a, b, (((0,), (0,)), ((), ())), preferred_element_type=F32)


def dot_nt(a, b):
    return lax.dot_general(a, b, (((1,), (1,)), ((), ())), preferred_element_type=F32)


def step_kernel(
    table_ref,
    indices_ref,
    momentum_ref,
    gradient_ref,
    weight_ref,
    tokens_ref,
    keys_ref,
    fresh_ref,
    moment_ref,
    table,
    moment,
    slope,
    waves,
    picks,
    packed,
    tokens_all,
    weight_mine,
    got,
    big,
    mid,
    small,
    total_acc,
    far_tokens,
    theirs,
    ours,
    block,
    local_sem,
    load_sem,
    send_sem,
    recv_sem,
):
    r, f = lax.axis_index("replica"), lax.axis_index("fsdp")
    x = lax.rem(f, 2) * 2 + r // 8
    y = lax.rem(r // 2, 4)
    z = f // 2
    c = lax.rem(r, 2)
    p, q = x + c * (y - x), y + c * (x - y)

    def device(p, q, z, c=c):
        x, y = p + c * (q - p), q + c * (p - q)
        return (lax.rem(x, 2) * 8 + y * 2 + c, z * 2 + x // 2)

    def around(value, step, size):
        return lax.rem(value + step + size, size)

    sibling = (r + 1 - 2 * c, f)
    z_peers = [(d, device(p, q, around(z, d, 8))) for d in range(1, 8)]
    p_peers = [(d, device(around(p, d, 4), q, z)) for d in range(1, 4)]
    q_peers = [(d, device(p, around(q, d, 4), z)) for d in range(1, 4)]
    group = [(d, (lax.rem(r + d, 16), f)) for d in range(1, 16)]
    x_far = [(lax.rem(r + d, 16), f + 1 - 2 * lax.rem(f, 2)) for d in (0, 8)]

    table_copy = pltpu.make_async_copy(table_ref, table, local_sem.at[4])
    table_copy.start()
    loads = []
    for part in range(4):
        rows = pl.ds(part * 128, 128)
        loads.append(
            (
                pltpu.make_async_copy(momentum_ref.at[rows], moment.at[rows], load_sem.at[part]),
                pltpu.make_async_copy(gradient_ref.at[rows], slope.at[rows], load_sem.at[4 + part]),
            )
        )
        for copy in loads[-1]:
            copy.start()
    g = lax.rem(x, 2) * 4 + y
    weight_copy = pltpu.make_async_copy(
        weight_ref.at[pl.ds(pl.multiple_of(g * BLOCK, BLOCK), BLOCK), pl.ds(pl.multiple_of(c * 512, 512), 512)],
        weight_mine,
        local_sem.at[1],
    )
    weight_copy.start()
    tokens_copy = pltpu.make_async_copy(tokens_ref, tokens_all.at[c], local_sem.at[2])
    tokens_copy.start()

    barrier = pltpu.get_barrier_semaphore()
    others = [peer for _, peer in z_peers + group] + x_far
    for peer in others:
        pl.semaphore_signal(barrier, inc=1, device_id=peer, device_id_type=MESH)

    started, whole = [], []
    count = [0]

    def lane():
        count[0] += 1
        return count[0] - 1

    def send(src, dst, slot, peer, keep=True):
        copy = pltpu.make_async_remote_copy(
            src_ref=src,
            dst_ref=dst,
            send_sem=send_sem.at[slot],
            recv_sem=recv_sem.at[slot],
            device_id=peer,
            device_id_type=MESH,
        )
        copy.start()
        if keep:
            started.append(copy)

    def receive(dst, slot):
        pltpu.make_async_remote_copy(
            src_ref=dst,
            dst_ref=dst,
            send_sem=send_sem.at[slot],
            recv_sem=recv_sem.at[slot],
            device_id=sibling,
            device_id_type=MESH,
        ).wait_recv()

    places = jnp.transpose(indices_ref[...].reshape(128, K).astype(F32)).astype(jnp.int32)
    lane_of = lax.broadcasted_iota(jnp.int32, (128, 128), 1)
    same = ((lax.broadcasted_iota(jnp.int32, (128, 128), 0) >> 5) & 1) == (lane_of >> 6)
    table_copy.wait()
    all_picks = jnp.zeros((128, 128), F32)
    all_places = jnp.zeros((128, 128), jnp.int32)
    for gx in range(8):
        if gx % 2 == 0:
            for copy in loads[gx // 2]:
                copy.wait()
        near, hots = [], []
        for quad in range(4):
            first = (gx * 4 + quad) * 4
            place = jnp.concatenate(
                [jnp.broadcast_to(places[:, first + i : first + i + 1], (K, 128)) for i in range(4)], axis=0
            )
            target = jnp.where(lane_of < BLOCK, place >> 6, (place & 63) + BLOCK)
            near.append(place)
            hots.append(jnp.where(target == lane_of, 1.0, 0.0).astype(BF16))
        all_chosen = jnp.dot(jnp.concatenate(hots, axis=0), table[:128], preferred_element_type=F32)
        for quad in range(4):
            unit = gx * 4 + quad
            rows, columns = pl.ds(gx * BLOCK, BLOCK), pl.ds(quad * QUAD, QUAD)
            place, chosen = near[quad], all_chosen[quad * 128 : quad * 128 + 128]
            waves[unit] = chosen.astype(BF16)
            moved = momentum_decay * moment[rows, columns] + slope[rows, columns].astype(F32)
            high, low = split(moved)
            three = jnp.concatenate([high, low, high], axis=0)
            chosen_row = chosen[:, :192].astype(BF16)
            partial = jnp.concatenate(
                [
                    jnp.dot(chosen_row[:BLOCK], three[:, :128], preferred_element_type=F32),
                    jnp.dot(chosen_row[BLOCK:], three[:, 128:], preferred_element_type=F32),
                ],
                axis=0,
            )
            terms = jnp.where(same, partial * (chosen[:, 256:384] + chosen[:, 384:]), 0.0)
            picked = jnp.broadcast_to(jnp.sum(terms, axis=1, keepdims=True), (128, 128))
            picks[unit] = picked[:, :BLOCK]
            all_picks = jnp.where(lane_of == unit, picked, all_picks)
            all_places = jnp.where(lane_of == unit, place, all_places)
    all_picks = jnp.transpose(all_picks)
    all_places = jnp.transpose(all_places.astype(F32))
    for unit in range(32):
        packed[unit // 2, unit % 2 : unit % 2 + 1] = all_picks[unit : unit + 1]
        packed[unit // 2, 2 + unit % 2 : 3 + unit % 2] = all_places[unit : unit + 1]

    pl.semaphore_wait(barrier, len(others))
    group_slots = [lane() for _ in group]
    for (d, peer), slot in zip(group, group_slots):
        send(packed.at[peer[0]], got.at[r], slot, peer)
    own_copy = pltpu.make_async_copy(packed.at[r], got.at[r], local_sem.at[0])
    own_copy.start()
    token_slot = lane()
    send(tokens_ref, tokens_all.at[c], token_slot, sibling)

    def leave(gx, carry):
        rows = pl.ds(pl.multiple_of(gx * BLOCK, BLOCK), BLOCK)
        for quad in range(4):
            unit, columns = gx * 4 + quad, pl.ds(quad * QUAD, QUAD)
            wave = waves[unit]
            row_wave = wave[:, :BLOCK].astype(F32) + wave[:, 128:192].astype(F32)
            high, low = split(row_wave * picks[unit])
            zero = jnp.zeros((), BF16)
            col_high, col_low = jnp.where(same, wave[:, 256:384], zero), jnp.where(same, wave[:, 384:], zero)
            back = []
            for pair in (slice(0, BLOCK), slice(BLOCK, 128)):
                back.append(
                    dot_tn(
                        jnp.concatenate([high[pair], high[pair], low[pair]], axis=0),
                        jnp.concatenate([col_high[pair], col_low[pair], col_high[pair]], axis=0),
                    )
                )
            back = jnp.concatenate(back, axis=1)
            moved = momentum_decay * moment[rows, columns] + slope[rows, columns].astype(F32)
            moment[rows, columns] = moved - back
        pltpu.make_async_copy(moment.at[rows], moment_ref.at[rows], local_sem.at[3]).start()
        return carry

    lax.fori_loop(0, 4, leave, 0)

    own_copy.wait()
    weight_copy.wait()

    freq = lax.broadcasted_iota(jnp.int32, (BLOCK, 128), 0)
    wide = lax.broadcasted_iota(jnp.int32, (QUAD, 128), 0)
    quarter = lax.broadcasted_iota(jnp.int32, (BLOCK, QUAD), 1) // BLOCK
    offset = (lax.broadcasted_iota(jnp.int32, (1, 128), 1) // K) * BLOCK
    fresh = []
    zero = jnp.zeros((), BF16)
    tile_high = jnp.concatenate([table[64:128, 256:384]] * 2, axis=1)
    tile_low = jnp.concatenate([table[64:128, 384:]] * 2, axis=1)
    across_high = jnp.concatenate([jnp.where(quarter == i, tile_high, zero) for i in range(4)], axis=0)
    across_low = jnp.concatenate([jnp.where(quarter == i, tile_low, zero) for i in range(4)], axis=0)
    across = jnp.concatenate([across_high, across_low, across_high], axis=0)
    sides = [([], [], []), ([], [], [])]
    for d in range(16):
        source = around(r, -d, 16)
        if d:
            receive(got.at[source], group_slots[d - 1])
        packet = got[source]
        for unit, (high, low, hot) in enumerate(sides):
            value = packet[unit : unit + 1, :]
            place = packet[2 + unit : 3 + unit, :].astype(jnp.int32)
            here = freq == place >> 6
            value_high, value_low = split(value)
            high.append(jnp.where(here, value_high.astype(F32), 0.0).astype(BF16))
            low.append(jnp.where(here, value_low.astype(F32), 0.0).astype(BF16))
            hot.append(jnp.where(wide == (place & 63) + offset, 1.0, 0.0).astype(BF16))
    for unit, (high, low, hot) in enumerate(sides):
        left = jnp.concatenate([jnp.concatenate(high, axis=1), jnp.concatenate(low, axis=1)], axis=0)
        both = dot_nt(left, jnp.concatenate(hot, axis=1))
        total = both[:BLOCK] + both[BLOCK:]
        high, low = split(total)
        inner = jnp.dot(
            table[128:, :192], jnp.concatenate([high, low, high], axis=0), preferred_element_type=F32
        )
        high, low = split(inner)
        update = jnp.dot(jnp.concatenate([high, high, low], axis=1), across, preferred_element_type=F32) / 16.0
        old = weight_mine[:, unit * QUAD : (unit + 1) * QUAD].astype(F32)
        fresh.append((old - step_size * update).astype(BF16))
    big[q, p, z] = fresh[0]
    mid[p, q, z] = fresh[1][:, :128]
    small[z, q, p] = fresh[1][:, 128:]

    p_next, p_last = p_peers[0][1], p_peers[2][1]
    q_next, q_last = q_peers[0][1], q_peers[2][1]
    z_next, z_last = z_peers[0][1], z_peers[6][1]
    small_1 = [lane() for _ in p_peers]
    mid_1 = [lane() for _ in z_peers]
    big_1 = [lane() for _ in z_peers]
    small_2 = [lane() for _ in q_peers]
    mid_2 = [lane() for _ in q_peers]
    big_2 = [lane() for _ in p_peers]
    mid_3 = [(lane(), lane()) for _ in range(4)]
    big_3 = [(lane(), lane()) for _ in range(4)]
    mid_4 = [lane() for _ in range(4)]
    big_4 = [lane() for _ in range(4)]
    small_3 = [[(lane(), lane()) for _ in range(2)] for _ in range(4)]
    near_first = [z_peers[d - 1] for d in (1, 7, 2, 6, 3, 5, 4)]

    mid_line = [(mid_3[0][0], p_next), (mid_3[0][1], p_last)] + [(mid_2[d - 1], q_peers[d - 1][1]) for d in (1, 3, 2)]
    big_line = [(big_3[0][0], q_next), (big_3[0][1], q_last)] + [(big_2[d - 1], p_peers[d - 1][1]) for d in (1, 3, 2)]
    for buffer, first, second, line in ((mid, p, q, mid_line), (big, q, p, big_line)):
        for slot, peer in line:
            whole.append((buffer.at[first, second], slot))

    def along(buffer, first, second, place, line):
        here = buffer.at[first, second, place]
        for slot, peer in line:
            send(here, here, slot, peer, keep=False)

    for (d, peer), slot in zip(p_peers, small_1):
        send(small.at[z, q, p], small.at[z, q, p], slot, peer)
    for d, peer in near_first:
        send(mid.at[p, q, z], mid.at[p, q, z], mid_1[d - 1], peer)
        send(big.at[q, p, z], big.at[q, p, z], big_1[d - 1], peer)
    along(mid, p, q, z, mid_line)
    along(big, q, p, z, big_line)

    lax.fori_loop(4, 8, leave, 0)

    for (d, peer), slot in zip(p_peers, small_1):
        receive(small.at[z, q, around(p, -d, 4)], slot)
    for (d, peer), slot in zip(q_peers, small_2):
        send(small.at[z, q], small.at[z, q], slot, peer)

    halves = [pl.ds(0, 2), pl.ds(2, 2)]
    for turn, (d, _) in enumerate(near_first):
        place = around(z, -d, 8)
        receive(mid.at[p, q, place], mid_1[d - 1])
        along(mid, p, q, place, mid_line)
        receive(big.at[q, p, place], big_1[d - 1])
        along(big, q, p, place, big_line)
        if turn == 3:
            for (d, peer), slot in zip(q_peers, small_2):
                receive(small.at[z, around(q, -d, 4)], slot)
            for half in range(2):
                send(small.at[z, halves[half]], small.at[z, halves[half]], small_3[0][half][0], z_next)
                send(small.at[z, halves[half]], small.at[z, halves[half]], small_3[0][half][1], z_last)

    p_far, q_far = around(p, 2, 4), around(q, 2, 4)
    tokens_copy.wait()
    receive(tokens_all.at[1 - c], token_slot)

    def piece(half, xi, yi, zi):
        start = pl.multiple_of(zi * 1024 + xi * 256 + (yi // 2) * 128, 128)
        return tokens_all[half, :, pl.ds(start, 128)]

    def line_up(i, carry):
        line, zi = i // 4, lax.rem(i, 4) * 2
        spot = pl.ds(pl.multiple_of(i * 128, 128), 128)
        for which, (pi, qi) in enumerate(((line, q_far), (p_far, line))):
            xi, yi = pi + c * (qi - pi), qi + c * (pi - qi)
            odd = lax.rem(yi, 2)

            def take(low):
                for half in range(2):
                    one, two = piece(half, xi, yi, zi), piece(half, xi, yi, zi + 1)
                    far_tokens[which, half, :, spot] = jnp.concatenate(
                        [one[:, low : low + BLOCK], two[:, low : low + BLOCK]], axis=1
                    )

            pl.when(odd == 0)(functools.partial(take, 0))
            pl.when(odd == 1)(functools.partial(take, BLOCK))
        return carry

    def small_step(step):
        before, after = around(z, -step, 8), around(z, step, 8)
        for half in range(2):
            receive(small.at[before, halves[half]], small_3[step - 1][half][0])
            if step < 3 or half == 0:
                here = small.at[before, halves[half]]
                send(here, here, small_3[step][half][0], z_next)
            receive(small.at[after, halves[half]], small_3[step - 1][half][1])
            if step < 3 or half == 1:
                here = small.at[after, halves[half]]
                send(here, here, small_3[step][half][1], z_last)

    for turn, d in enumerate((1, 3, 2)):
        here = mid.at[p, around(q, -d, 4)]
        receive(here, mid_2[d - 1])
        send(here, here, mid_3[d][0], p_next)
        send(here, here, mid_3[d][1], p_last)
        here = big.at[q, around(p, -d, 4)]
        receive(here, big_2[d - 1])
        send(here, here, big_3[d][0], q_next)
        send(here, here, big_3[d][1], q_last)
        if turn == 1:
            small_step(1)

    small_step(2)
    for turn, d in enumerate((0, 1, 3, 2)):
        for buffer, slots, onward, first, second, ahead, behind in (
            (mid, mid_3, mid_4, p, q, p_next, p_last),
            (big, big_3, big_4, q, p, q_next, q_last),
        ):
            sub = around(second, -d, 4)
            left = buffer.at[around(first, -1, 4), sub]
            right = buffer.at[around(first, 1, 4), sub]
            receive(left, slots[d][0])
            if d in (0, 2):
                send(left, left, onward[d], ahead)
            receive(right, slots[d][1])
            if d in (1, 3):
                send(right, right, onward[d], behind)
        if turn == 2:
            small_step(3)
        if turn < 3:
            lax.fori_loop((0, 6, 11)[turn], (6, 11, 16)[turn], line_up, 0)

    opposite = around(z, 4, 8)
    total_acc[...] = jnp.zeros_like(total_acc)

    def known_rows(zi, xi, yi):
        pi, qi = xi + c * (yi - xi), yi + c * (xi - yi)
        none = jnp.zeros((), BF16)
        pw = pi + (p - pi) * (pi == p_far).astype(jnp.int32)
        qw = qi + (q - qi) * (qi == q_far).astype(jnp.int32)
        zw = zi + (z - zi) * (zi == opposite).astype(jnp.int32)
        return jnp.concatenate(
            [
                jnp.where(qi == q_far, none, big[qw, pi, zi]),
                jnp.where(pi == p_far, none, mid[pw, qi, zi]),
                jnp.where(zi == opposite, none, small[zw, qi, pi]),
            ],
            axis=1,
        )

    def multiply(zi, carry):
        right = jnp.concatenate([known_rows(zi, xi, yi) for xi in range(4) for yi in range(4)], axis=0)
        depth = pl.ds(pl.multiple_of(zi * 1024, 1024), 1024)
        for half in range(2):
            total_acc[half] += jnp.dot(tokens_all[half, :, depth], right, preferred_element_type=F32)
        return carry

    lax.fori_loop(0, 8, multiply, 0)

    for d in (0, 1, 3, 2):
        receive(mid.at[around(p, 2, 4), around(q, -d, 4)], mid_4[d])
        receive(big.at[around(q, 2, 4), around(p, -d, 4)], big_4[d])
    receive(small.at[opposite, halves[0]], small_3[3][0][0])
    receive(small.at[opposite, halves[1]], small_3[3][1][1])

    weight_slot = lane()
    keys_slot = lane()

    def rows_of(zi, xi, yi):
        pi, qi = xi + c * (yi - xi), yi + c * (xi - yi)
        return jnp.concatenate([big[qi, pi, zi], mid[pi, qi, zi], small[zi, qi, pi]], axis=1)

    x_high = 2 * lax.rem(f, 2)
    for xi in range(2):
        for yi in range(4):
            block[xi * 4 + yi] = rows_of(z, x_high + xi, yi)
    send(block, fresh_ref.at[c], weight_slot, sibling)
    block_copy = pltpu.make_async_copy(block, fresh_ref.at[c], local_sem.at[0])
    block_copy.start()

    far_small = jnp.concatenate(
        [
            small[opposite, yi + c * (xi - yi), xi + c * (yi - xi)]
            for xi in range(4)
            for yi in range(4)
        ],
        axis=0,
    )
    depth = pl.ds(pl.multiple_of(opposite * 1024, 1024), 1024)

    def finish(half):
        sums = jnp.concatenate(
            [
                jnp.dot(far_tokens[0, half], big[q_far].reshape(2048, 256), preferred_element_type=F32),
                jnp.dot(far_tokens[1, half], mid[p_far].reshape(2048, 128), preferred_element_type=F32),
                jnp.dot(tokens_all[half, :, depth], far_small, preferred_element_type=F32),
            ],
            axis=1,
        )
        return (total_acc[half] + sums).astype(BF16)

    theirs[...] = finish(1 - c)
    send(theirs, keys_ref.at[c], keys_slot, sibling)
    ours[...] = finish(c)
    keys_copy = pltpu.make_async_copy(ours, keys_ref.at[c], local_sem.at[1])
    keys_copy.start()
    block_copy.wait()
    keys_copy.wait()
    receive(fresh_ref.at[1 - c], weight_slot)
    receive(keys_ref.at[1 - c], keys_slot)
    pltpu.make_async_copy(moment, moment_ref, local_sem.at[3]).wait()
    for copy in started:
        copy.wait_send()
    for line, slot in whole:
        pltpu.make_async_remote_copy(
            src_ref=line,
            dst_ref=line,
            send_sem=send_sem.at[slot],
            recv_sem=recv_sem.at[slot],
            device_id=sibling,
            device_id_type=MESH,
        ).wait_send()


def step(table, indices, momentum, gradient, weight, tokens):
    vmem = pl.BlockSpec(memory_space=pltpu.VMEM)
    hbm = pl.BlockSpec(memory_space=pl.ANY)
    slots = 128
    return pl.pallas_call(
        step_kernel,
        in_specs=[hbm, vmem, hbm, hbm, hbm, hbm],
        out_specs=[hbm, hbm, hbm],
        out_shape=[
            jax.ShapeDtypeStruct((2, 256, 512), BF16),
            jax.ShapeDtypeStruct((2, 8, 64, 512), BF16),
            jax.ShapeDtypeStruct((512, 1024), F32),
        ],
        scratch_shapes=[
            pltpu.VMEM((192, 512), BF16),
            pltpu.VMEM((512, 1024), F32),
            pltpu.VMEM((512, 1024), BF16),
            pltpu.VMEM((32, 128, 512), BF16),
            pltpu.VMEM((32, 128, 64), F32),
            pltpu.VMEM((16, 8, 128), F32),
            pltpu.VMEM((2, 256, 8192), BF16),
            pltpu.VMEM((64, 512), BF16),
            pltpu.VMEM((16, 8, 128), F32),
            pltpu.VMEM((4, 4, 8, 64, 256), BF16),
            pltpu.VMEM((4, 4, 8, 64, 128), BF16),
            pltpu.VMEM((8, 4, 4, 64, 128), BF16),
            pltpu.VMEM((2, 256, 512), F32),
            pltpu.VMEM((2, 2, 256, 2048), BF16),
            pltpu.VMEM((256, 512), BF16),
            pltpu.VMEM((256, 512), BF16),
            pltpu.VMEM((8, 64, 512), BF16),
            pltpu.SemaphoreType.DMA((5,)),
            pltpu.SemaphoreType.DMA((8,)),
            pltpu.SemaphoreType.DMA((slots,)),
            pltpu.SemaphoreType.DMA((slots,)),
        ],
        compiler_params=pltpu.CompilerParams(collective_id=0, has_side_effects=True, vmem_limit_bytes=60 * 2**20),
    )(table, indices, momentum, gradient, weight, tokens)


def place_kernel(keys_in, fresh_in, moment_in, keys_out, fresh_out, moment_out, keys, fresh, moment, in_sem, out_sem):
    moves = []
    for half in range(2):
        columns = pl.ds(half * 512, 512)
        for part in range(2):
            rows = pl.ds(part * 128, 128)
            moves.append((keys_in.at[half, rows], keys.at[half, rows], keys_out.at[rows, columns]))
        for part in range(4):
            rows = pl.ds(part * 128, 128)
            moves.append((fresh_in.at[half, rows], fresh.at[half, rows], fresh_out.at[rows, columns]))
    for part in range(8):
        rows = pl.ds(part * 64, 64)
        moves.append((moment_in.at[rows], moment.at[rows], moment_out.at[rows]))
    ins = [pltpu.make_async_copy(a, b, in_sem.at[i]) for i, (a, b, _) in enumerate(moves)]
    outs = [pltpu.make_async_copy(b, o, out_sem.at[i]) for i, (_, b, o) in enumerate(moves)]
    for copy in ins:
        copy.start()
    for copy, onward in zip(ins, outs):
        copy.wait()
        onward.start()
    for copy in outs:
        copy.wait()


def put_in_place(keys, fresh, moment):
    hbm = pl.BlockSpec(memory_space=pl.ANY)
    return pl.pallas_call(
        place_kernel,
        in_specs=[hbm] * 3,
        out_specs=[hbm] * 3,
        out_shape=[
            jax.ShapeDtypeStruct((256, 1024), BF16),
            jax.ShapeDtypeStruct((512, 1024), BF16),
            jax.ShapeDtypeStruct((512, 1024), F32),
        ],
        scratch_shapes=[
            pltpu.VMEM((2, 256, 512), BF16),
            pltpu.VMEM((2, 512, 512), BF16),
            pltpu.VMEM((512, 1024), F32),
            pltpu.SemaphoreType.DMA((20,)),
            pltpu.SemaphoreType.DMA((20,)),
        ],
        compiler_params=pltpu.CompilerParams(vmem_limit_bytes=63 * 2**20),
    )(keys, fresh, moment)


def per_device(tokens, weight, momentum, gradient, indices):
    keys, fresh, moment = step(jnp.asarray(tables()), indices[0], momentum[0], gradient[0], weight, tokens)
    keys, fresh, moment = put_in_place(keys, fresh.reshape(2, 512, 512), moment)
    return (keys, fresh, moment[None])


def solution(mesh):
    return jax.shard_map(
        per_device,
        mesh=mesh,
        in_specs=(
            P(("replica", "fsdp"), None),
            P("fsdp", None),
            P("replica", "fsdp", None),
            P("replica", "fsdp", None),
            P("replica", "fsdp", None, None),
        ),
        out_specs=(P(("replica", "fsdp"), None), P("fsdp", None), P("replica", "fsdp", None)),
        check_vma=False,
    )
```

```python
import functools

import jax
import jax.numpy as jnp
import ml_dtypes
import numpy as np
from jax import lax
from jax.experimental import pallas as pl
from jax.experimental.pallas import tpu as pltpu
from jax.sharding import PartitionSpec as P

BLOCK = 64
K = 32
QUAD = 256
MESH = pl.DeviceIdType.MESH
F32 = jnp.float32
BF16 = jnp.bfloat16

momentum_decay = 0.9
step_size = 0.1


def dct_table(size):
    freq = np.arange(size, dtype=np.float64)[:, None]
    place = np.arange(size, dtype=np.float64)[None, :]
    scale = np.where(freq == 0, np.sqrt(1.0 / size), np.sqrt(2.0 / size))
    return (scale * np.cos(np.pi * (2.0 * place + 1.0) * freq / (2.0 * size))).astype(np.float32)


def tables():
    table = dct_table(BLOCK)
    high = table.astype(ml_dtypes.bfloat16)
    low = (table - high.astype(np.float32)).astype(ml_dtypes.bfloat16)
    out = np.zeros((192, 512), ml_dtypes.bfloat16)
    out[:64, :192] = np.concatenate([high, high, low], axis=1)
    out[64:128, 256:384] = np.tile(high, (1, 2))
    out[64:128, 384:512] = np.tile(low, (1, 2))
    out[128:, :192] = np.concatenate([high.T, high.T, low.T], axis=1)
    return out


def split(value):
    high = value.astype(BF16)
    return high, (value - high.astype(F32)).astype(BF16)


def dot_tn(a, b):
    return lax.dot_general(a, b, (((0,), (0,)), ((), ())), preferred_element_type=F32)


def dot_nt(a, b):
    return lax.dot_general(a, b, (((1,), (1,)), ((), ())), preferred_element_type=F32)


def step_kernel(
    table_ref,
    indices_ref,
    momentum_ref,
    gradient_ref,
    weight_ref,
    tokens_ref,
    keys_ref,
    fresh_ref,
    moment_ref,
    table,
    moment,
    slope,
    waves,
    picks,
    packed,
    tokens_all,
    weight_mine,
    got,
    big,
    mid,
    small,
    total_acc,
    far_tokens,
    theirs,
    ours,
    block,
    local_sem,
    load_sem,
    send_sem,
    recv_sem,
):
    r, f = lax.axis_index("replica"), lax.axis_index("fsdp")
    x = lax.rem(f, 2) * 2 + r // 8
    y = lax.rem(r // 2, 4)
    z = f // 2
    c = lax.rem(r, 2)
    p, q = x + c * (y - x), y + c * (x - y)

    def device(p, q, z, c=c):
        x, y = p + c * (q - p), q + c * (p - q)
        return (lax.rem(x, 2) * 8 + y * 2 + c, z * 2 + x // 2)

    def around(value, step, size):
        return lax.rem(value + step + size, size)

    sibling = (r + 1 - 2 * c, f)
    z_peers = [(d, device(p, q, around(z, d, 8))) for d in range(1, 8)]
    p_peers = [(d, device(around(p, d, 4), q, z)) for d in range(1, 4)]
    q_peers = [(d, device(p, around(q, d, 4), z)) for d in range(1, 4)]
    group = [(d, (lax.rem(r + d, 16), f)) for d in range(1, 16)]
    x_far = [(lax.rem(r + d, 16), f + 1 - 2 * lax.rem(f, 2)) for d in (0, 8)]

    table_copy = pltpu.make_async_copy(table_ref, table, local_sem.at[4])
    table_copy.start()
    loads = []
    for part in range(4):
        rows = pl.ds(part * 128, 128)
        loads.append(
            (
                pltpu.make_async_copy(momentum_ref.at[rows], moment.at[rows], load_sem.at[part]),
                pltpu.make_async_copy(gradient_ref.at[rows], slope.at[rows], load_sem.at[4 + part]),
            )
        )
        for copy in loads[-1]:
            copy.start()
    g = lax.rem(x, 2) * 4 + y
    weight_copy = pltpu.make_async_copy(
        weight_ref.at[pl.ds(pl.multiple_of(g * BLOCK, BLOCK), BLOCK), pl.ds(pl.multiple_of(c * 512, 512), 512)],
        weight_mine,
        local_sem.at[1],
    )
    weight_copy.start()
    tokens_copy = pltpu.make_async_copy(tokens_ref, tokens_all.at[c], local_sem.at[2])
    tokens_copy.start()

    barrier = pltpu.get_barrier_semaphore()
    others = [peer for _, peer in z_peers + group] + x_far
    for peer in others:
        pl.semaphore_signal(barrier, inc=1, device_id=peer, device_id_type=MESH)

    started, whole = [], []
    count = [0]

    def lane():
        count[0] += 1
        return count[0] - 1

    def send(src, dst, slot, peer, keep=True):
        copy = pltpu.make_async_remote_copy(
            src_ref=src,
            dst_ref=dst,
            send_sem=send_sem.at[slot],
            recv_sem=recv_sem.at[slot],
            device_id=peer,
            device_id_type=MESH,
        )
        copy.start()
        if keep:
            started.append(copy)

    def receive(dst, slot):
        pltpu.make_async_remote_copy(
            src_ref=dst,
            dst_ref=dst,
            send_sem=send_sem.at[slot],
            recv_sem=recv_sem.at[slot],
            device_id=sibling,
            device_id_type=MESH,
        ).wait_recv()

    places = jnp.transpose(indices_ref[...].reshape(128, K).astype(F32)).astype(jnp.int32)
    lane_of = lax.broadcasted_iota(jnp.int32, (128, 128), 1)
    same = ((lax.broadcasted_iota(jnp.int32, (128, 128), 0) >> 5) & 1) == (lane_of >> 6)
    table_copy.wait()
    all_picks = jnp.zeros((128, 128), F32)
    all_places = jnp.zeros((128, 128), jnp.int32)
    for gx in range(8):
        hots = []
        for quad in range(4):
            unit = gx * 4 + quad
            place = jnp.concatenate(
                [jnp.broadcast_to(places[:, unit * 4 + i : unit * 4 + i + 1], (K, 128)) for i in range(4)], axis=0
            )
            target = jnp.where(lane_of < BLOCK, place >> 6, (place & 63) + BLOCK)
            all_places = jnp.where(lane_of == unit, place, all_places)
            hots.append(jnp.where(target == lane_of, 1.0, 0.0).astype(BF16))
        chosen = jnp.dot(jnp.concatenate(hots, axis=0), table[:128], preferred_element_type=F32).astype(BF16)
        for quad in range(4):
            waves[gx * 4 + quad] = chosen[quad * 128 : quad * 128 + 128]
    for gx in range(8):
        if gx % 2 == 0:
            for copy in loads[gx // 2]:
                copy.wait()
        for quad in range(4):
            unit = gx * 4 + quad
            rows, columns = pl.ds(gx * BLOCK, BLOCK), pl.ds(quad * QUAD, QUAD)
            wave = waves[unit]
            moved = momentum_decay * moment[rows, columns] + slope[rows, columns].astype(F32)
            high, low = split(moved)
            three = jnp.concatenate([high, low, high], axis=0)
            partial = jnp.concatenate(
                [
                    jnp.dot(wave[:BLOCK, :192], three[:, :128], preferred_element_type=F32),
                    jnp.dot(wave[BLOCK:, :192], three[:, 128:], preferred_element_type=F32),
                ],
                axis=0,
            )
            terms = jnp.where(same, partial * (wave[:, 256:384].astype(F32) + wave[:, 384:].astype(F32)), 0.0)
            picked = jnp.broadcast_to(jnp.sum(terms, axis=1, keepdims=True), (128, 128))
            picks[unit] = picked[:, :BLOCK]
            all_picks = jnp.where(lane_of == unit, picked, all_picks)
    all_picks = jnp.transpose(all_picks)
    all_places = jnp.transpose(all_places.astype(F32))
    for unit in range(32):
        packed[unit // 2, unit % 2 : unit % 2 + 1] = all_picks[unit : unit + 1]
        packed[unit // 2, 2 + unit % 2 : 3 + unit % 2] = all_places[unit : unit + 1]

    pl.semaphore_wait(barrier, len(others))
    group_slots = [lane() for _ in group]
    for (d, peer), slot in zip(group, group_slots):
        send(packed.at[peer[0]], got.at[r], slot, peer)
    own_copy = pltpu.make_async_copy(packed.at[r], got.at[r], local_sem.at[0])
    own_copy.start()
    token_slot = lane()
    send(tokens_ref, tokens_all.at[c], token_slot, sibling)

    def leave(gx, carry):
        rows = pl.ds(pl.multiple_of(gx * BLOCK, BLOCK), BLOCK)
        for quad in range(4):
            unit, columns = gx * 4 + quad, pl.ds(quad * QUAD, QUAD)
            wave = waves[unit]
            row_wave = wave[:, :BLOCK].astype(F32) + wave[:, 128:192].astype(F32)
            high, low = split(row_wave * picks[unit])
            zero = jnp.zeros((), BF16)
            col_high, col_low = jnp.where(same, wave[:, 256:384], zero), jnp.where(same, wave[:, 384:], zero)
            back = []
            for pair in (slice(0, BLOCK), slice(BLOCK, 128)):
                back.append(
                    dot_tn(
                        jnp.concatenate([high[pair], high[pair], low[pair]], axis=0),
                        jnp.concatenate([col_high[pair], col_low[pair], col_high[pair]], axis=0),
                    )
                )
            back = jnp.concatenate(back, axis=1)
            moved = momentum_decay * moment[rows, columns] + slope[rows, columns].astype(F32)
            moment[rows, columns] = moved - back
        pltpu.make_async_copy(moment.at[rows], moment_ref.at[rows], local_sem.at[3]).start()
        return carry

    lax.fori_loop(0, 4, leave, 0)

    own_copy.wait()
    weight_copy.wait()

    freq = lax.broadcasted_iota(jnp.int32, (BLOCK, 128), 0)
    wide = lax.broadcasted_iota(jnp.int32, (QUAD, 128), 0)
    quarter = lax.broadcasted_iota(jnp.int32, (BLOCK, QUAD), 1) // BLOCK
    offset = (lax.broadcasted_iota(jnp.int32, (1, 128), 1) // K) * BLOCK
    fresh = []
    zero = jnp.zeros((), BF16)
    tile_high = jnp.concatenate([table[64:128, 256:384]] * 2, axis=1)
    tile_low = jnp.concatenate([table[64:128, 384:]] * 2, axis=1)
    across_high = jnp.concatenate([jnp.where(quarter == i, tile_high, zero) for i in range(4)], axis=0)
    across_low = jnp.concatenate([jnp.where(quarter == i, tile_low, zero) for i in range(4)], axis=0)
    across = jnp.concatenate([across_high, across_low, across_high], axis=0)
    sides = [([], [], []), ([], [], [])]
    for d in range(16):
        source = around(r, -d, 16)
        if d:
            receive(got.at[source], group_slots[d - 1])
        packet = got[source]
        for unit, (high, low, hot) in enumerate(sides):
            value = packet[unit : unit + 1, :]
            place = packet[2 + unit : 3 + unit, :].astype(jnp.int32)
            here = freq == place >> 6
            value_high, value_low = split(value)
            high.append(jnp.where(here, value_high.astype(F32), 0.0).astype(BF16))
            low.append(jnp.where(here, value_low.astype(F32), 0.0).astype(BF16))
            hot.append(jnp.where(wide == (place & 63) + offset, 1.0, 0.0).astype(BF16))
    for unit, (high, low, hot) in enumerate(sides):
        left = jnp.concatenate([jnp.concatenate(high, axis=1), jnp.concatenate(low, axis=1)], axis=0)
        both = dot_nt(left, jnp.concatenate(hot, axis=1))
        total = both[:BLOCK] + both[BLOCK:]
        high, low = split(total)
        inner = jnp.dot(
            table[128:, :192], jnp.concatenate([high, low, high], axis=0), preferred_element_type=F32
        )
        high, low = split(inner)
        update = jnp.dot(jnp.concatenate([high, high, low], axis=1), across, preferred_element_type=F32) / 16.0
        old = weight_mine[:, unit * QUAD : (unit + 1) * QUAD].astype(F32)
        fresh.append((old - step_size * update).astype(BF16))
    big[q, p, z] = fresh[0]
    mid[p, q, z] = fresh[1][:, :128]
    small[z, q, p] = fresh[1][:, 128:]

    p_next, p_last = p_peers[0][1], p_peers[2][1]
    q_next, q_last = q_peers[0][1], q_peers[2][1]
    z_next, z_last = z_peers[0][1], z_peers[6][1]
    small_1 = [lane() for _ in p_peers]
    mid_1 = [lane() for _ in z_peers]
    big_1 = [lane() for _ in z_peers]
    small_2 = [lane() for _ in q_peers]
    mid_2 = [lane() for _ in q_peers]
    big_2 = [lane() for _ in p_peers]
    mid_3 = [(lane(), lane()) for _ in range(4)]
    big_3 = [(lane(), lane()) for _ in range(4)]
    mid_4 = [lane() for _ in range(4)]
    big_4 = [lane() for _ in range(4)]
    small_3 = [[(lane(), lane()) for _ in range(2)] for _ in range(4)]
    near_first = [z_peers[d - 1] for d in (1, 7, 2, 6, 3, 5, 4)]

    mid_line = [(mid_3[0][0], p_next), (mid_3[0][1], p_last)] + [(mid_2[d - 1], q_peers[d - 1][1]) for d in (1, 3, 2)]
    big_line = [(big_3[0][0], q_next), (big_3[0][1], q_last)] + [(big_2[d - 1], p_peers[d - 1][1]) for d in (1, 3, 2)]
    for buffer, first, second, line in ((mid, p, q, mid_line), (big, q, p, big_line)):
        for slot, peer in line:
            whole.append((buffer.at[first, second], slot))

    def along(buffer, first, second, place, line):
        here = buffer.at[first, second, place]
        for slot, peer in line:
            send(here, here, slot, peer, keep=False)

    for (d, peer), slot in zip(p_peers, small_1):
        send(small.at[z, q, p], small.at[z, q, p], slot, peer)
    for d, peer in near_first:
        send(mid.at[p, q, z], mid.at[p, q, z], mid_1[d - 1], peer)
        send(big.at[q, p, z], big.at[q, p, z], big_1[d - 1], peer)
    along(mid, p, q, z, mid_line)
    along(big, q, p, z, big_line)

    lax.fori_loop(4, 8, leave, 0)

    for (d, peer), slot in zip(p_peers, small_1):
        receive(small.at[z, q, around(p, -d, 4)], slot)
    for (d, peer), slot in zip(q_peers, small_2):
        send(small.at[z, q], small.at[z, q], slot, peer)

    halves = [pl.ds(0, 2), pl.ds(2, 2)]
    for turn, (d, _) in enumerate(near_first):
        place = around(z, -d, 8)
        receive(mid.at[p, q, place], mid_1[d - 1])
        along(mid, p, q, place, mid_line)
        receive(big.at[q, p, place], big_1[d - 1])
        along(big, q, p, place, big_line)
        if turn == 3:
            for (d, peer), slot in zip(q_peers, small_2):
                receive(small.at[z, around(q, -d, 4)], slot)
            for half in range(2):
                send(small.at[z, halves[half]], small.at[z, halves[half]], small_3[0][half][0], z_next)
                send(small.at[z, halves[half]], small.at[z, halves[half]], small_3[0][half][1], z_last)

    p_far, q_far = around(p, 2, 4), around(q, 2, 4)
    tokens_copy.wait()
    receive(tokens_all.at[1 - c], token_slot)

    def piece(half, xi, yi, zi):
        start = pl.multiple_of(zi * 1024 + xi * 256 + (yi // 2) * 128, 128)
        return tokens_all[half, :, pl.ds(start, 128)]

    def line_up(i, carry):
        line, zi = i // 4, lax.rem(i, 4) * 2
        spot = pl.ds(pl.multiple_of(i * 128, 128), 128)
        for which, (pi, qi) in enumerate(((line, q_far), (p_far, line))):
            xi, yi = pi + c * (qi - pi), qi + c * (pi - qi)
            odd = lax.rem(yi, 2)

            def take(low):
                for half in range(2):
                    one, two = piece(half, xi, yi, zi), piece(half, xi, yi, zi + 1)
                    far_tokens[which, half, :, spot] = jnp.concatenate(
                        [one[:, low : low + BLOCK], two[:, low : low + BLOCK]], axis=1
                    )

            pl.when(odd == 0)(functools.partial(take, 0))
            pl.when(odd == 1)(functools.partial(take, BLOCK))
        return carry

    def small_step(step):
        before, after = around(z, -step, 8), around(z, step, 8)
        for half in range(2):
            receive(small.at[before, halves[half]], small_3[step - 1][half][0])
            if step < 3 or half == 0:
                here = small.at[before, halves[half]]
                send(here, here, small_3[step][half][0], z_next)
            receive(small.at[after, halves[half]], small_3[step - 1][half][1])
            if step < 3 or half == 1:
                here = small.at[after, halves[half]]
                send(here, here, small_3[step][half][1], z_last)

    for turn, d in enumerate((1, 3, 2)):
        here = mid.at[p, around(q, -d, 4)]
        receive(here, mid_2[d - 1])
        send(here, here, mid_3[d][0], p_next)
        send(here, here, mid_3[d][1], p_last)
        here = big.at[q, around(p, -d, 4)]
        receive(here, big_2[d - 1])
        send(here, here, big_3[d][0], q_next)
        send(here, here, big_3[d][1], q_last)
        if turn == 1:
            small_step(1)

    small_step(2)
    for turn, d in enumerate((0, 1, 3, 2)):
        for buffer, slots, onward, first, second, ahead, behind in (
            (mid, mid_3, mid_4, p, q, p_next, p_last),
            (big, big_3, big_4, q, p, q_next, q_last),
        ):
            sub = around(second, -d, 4)
            left = buffer.at[around(first, -1, 4), sub]
            right = buffer.at[around(first, 1, 4), sub]
            receive(left, slots[d][0])
            if d in (0, 2):
                send(left, left, onward[d], ahead)
            receive(right, slots[d][1])
            if d in (1, 3):
                send(right, right, onward[d], behind)
        if turn == 2:
            small_step(3)
        if turn < 3:
            lax.fori_loop((0, 6, 11)[turn], (6, 11, 16)[turn], line_up, 0)

    opposite = around(z, 4, 8)
    total_acc[...] = jnp.zeros_like(total_acc)

    def known_rows(zi, xi, yi):
        pi, qi = xi + c * (yi - xi), yi + c * (xi - yi)
        none = jnp.zeros((), BF16)
        pw = pi + (p - pi) * (pi == p_far).astype(jnp.int32)
        qw = qi + (q - qi) * (qi == q_far).astype(jnp.int32)
        zw = zi + (z - zi) * (zi == opposite).astype(jnp.int32)
        return jnp.concatenate(
            [
                jnp.where(qi == q_far, none, big[qw, pi, zi]),
                jnp.where(pi == p_far, none, mid[pw, qi, zi]),
                jnp.where(zi == opposite, none, small[zw, qi, pi]),
            ],
            axis=1,
        )

    def multiply(zi, carry):
        right = jnp.concatenate([known_rows(zi, xi, yi) for xi in range(4) for yi in range(4)], axis=0)
        depth = pl.ds(pl.multiple_of(zi * 1024, 1024), 1024)
        for half in range(2):
            total_acc[half] += jnp.dot(tokens_all[half, :, depth], right, preferred_element_type=F32)
        return carry

    lax.fori_loop(0, 8, multiply, 0)

    for d in (0, 1, 3, 2):
        receive(mid.at[around(p, 2, 4), around(q, -d, 4)], mid_4[d])
        receive(big.at[around(q, 2, 4), around(p, -d, 4)], big_4[d])
    receive(small.at[opposite, halves[0]], small_3[3][0][0])
    receive(small.at[opposite, halves[1]], small_3[3][1][1])

    weight_slot = lane()
    keys_slot = lane()

    def rows_of(zi, xi, yi):
        pi, qi = xi + c * (yi - xi), yi + c * (xi - yi)
        return jnp.concatenate([big[qi, pi, zi], mid[pi, qi, zi], small[zi, qi, pi]], axis=1)

    x_high = 2 * lax.rem(f, 2)
    for xi in range(2):
        for yi in range(4):
            block[xi * 4 + yi] = rows_of(z, x_high + xi, yi)
    send(block, fresh_ref.at[c], weight_slot, sibling)
    block_copy = pltpu.make_async_copy(block, fresh_ref.at[c], local_sem.at[0])
    block_copy.start()

    far_small = jnp.concatenate(
        [
            small[opposite, yi + c * (xi - yi), xi + c * (yi - xi)]
            for xi in range(4)
            for yi in range(4)
        ],
        axis=0,
    )
    depth = pl.ds(pl.multiple_of(opposite * 1024, 1024), 1024)

    def finish(half):
        sums = jnp.concatenate(
            [
                jnp.dot(far_tokens[0, half], big[q_far].reshape(2048, 256), preferred_element_type=F32),
                jnp.dot(far_tokens[1, half], mid[p_far].reshape(2048, 128), preferred_element_type=F32),
                jnp.dot(tokens_all[half, :, depth], far_small, preferred_element_type=F32),
            ],
            axis=1,
        )
        return (total_acc[half] + sums).astype(BF16)

    theirs[...] = finish(1 - c)
    send(theirs, keys_ref.at[c], keys_slot, sibling)
    ours[...] = finish(c)
    keys_copy = pltpu.make_async_copy(ours, keys_ref.at[c], local_sem.at[1])
    keys_copy.start()
    block_copy.wait()
    keys_copy.wait()
    receive(fresh_ref.at[1 - c], weight_slot)
    receive(keys_ref.at[1 - c], keys_slot)
    pltpu.make_async_copy(moment, moment_ref, local_sem.at[3]).wait()
    for copy in started:
        copy.wait_send()
    for line, slot in whole:
        pltpu.make_async_remote_copy(
            src_ref=line,
            dst_ref=line,
            send_sem=send_sem.at[slot],
            recv_sem=recv_sem.at[slot],
            device_id=sibling,
            device_id_type=MESH,
        ).wait_send()


def step(table, indices, momentum, gradient, weight, tokens):
    vmem = pl.BlockSpec(memory_space=pltpu.VMEM)
    hbm = pl.BlockSpec(memory_space=pl.ANY)
    slots = 128
    return pl.pallas_call(
        step_kernel,
        in_specs=[hbm, vmem, hbm, hbm, hbm, hbm],
        out_specs=[hbm, hbm, hbm],
        out_shape=[
            jax.ShapeDtypeStruct((2, 256, 512), BF16),
            jax.ShapeDtypeStruct((2, 8, 64, 512), BF16),
            jax.ShapeDtypeStruct((512, 1024), F32),
        ],
        scratch_shapes=[
            pltpu.VMEM((192, 512), BF16),
            pltpu.VMEM((512, 1024), F32),
            pltpu.VMEM((512, 1024), BF16),
            pltpu.VMEM((32, 128, 512), BF16),
            pltpu.VMEM((32, 128, 64), F32),
            pltpu.VMEM((16, 8, 128), F32),
            pltpu.VMEM((2, 256, 8192), BF16),
            pltpu.VMEM((64, 512), BF16),
            pltpu.VMEM((16, 8, 128), F32),
            pltpu.VMEM((4, 4, 8, 64, 256), BF16),
            pltpu.VMEM((4, 4, 8, 64, 128), BF16),
            pltpu.VMEM((8, 4, 4, 64, 128), BF16),
            pltpu.VMEM((2, 256, 512), F32),
            pltpu.VMEM((2, 2, 256, 2048), BF16),
            pltpu.VMEM((256, 512), BF16),
            pltpu.VMEM((256, 512), BF16),
            pltpu.VMEM((8, 64, 512), BF16),
            pltpu.SemaphoreType.DMA((5,)),
            pltpu.SemaphoreType.DMA((8,)),
            pltpu.SemaphoreType.DMA((slots,)),
            pltpu.SemaphoreType.DMA((slots,)),
        ],
        compiler_params=pltpu.CompilerParams(collective_id=0, has_side_effects=True, vmem_limit_bytes=60 * 2**20),
    )(table, indices, momentum, gradient, weight, tokens)


def place_kernel(keys_in, fresh_in, moment_in, keys_out, fresh_out, moment_out, keys, fresh, moment, in_sem, out_sem):
    moves = []
    for part in range(4):
        rows = pl.ds(part * 128, 128)
        moves.append((moment_in.at[rows], moment.at[rows], moment_out.at[rows]))
    for half in range(2):
        columns = pl.ds(half * 512, 512)
        for part in range(1):
            rows = pl.ds(0, 256)
            moves.append((keys_in.at[half, rows], keys.at[half, rows], keys_out.at[rows, columns]))
        for part in range(2):
            rows = pl.ds(part * 256, 256)
            moves.append((fresh_in.at[half, rows], fresh.at[half, rows], fresh_out.at[rows, columns]))
    ins = [pltpu.make_async_copy(a, b, in_sem.at[i]) for i, (a, b, _) in enumerate(moves)]
    outs = [pltpu.make_async_copy(b, o, out_sem.at[i]) for i, (_, b, o) in enumerate(moves)]
    for copy in ins:
        copy.start()
    for copy, onward in zip(ins, outs):
        copy.wait()
        onward.start()
    for copy in outs:
        copy.wait()


def put_in_place(keys, fresh, moment):
    hbm = pl.BlockSpec(memory_space=pl.ANY)
    return pl.pallas_call(
        place_kernel,
        in_specs=[hbm] * 3,
        out_specs=[hbm] * 3,
        out_shape=[
            jax.ShapeDtypeStruct((256, 1024), BF16),
            jax.ShapeDtypeStruct((512, 1024), BF16),
            jax.ShapeDtypeStruct((512, 1024), F32),
        ],
        scratch_shapes=[
            pltpu.VMEM((2, 256, 512), BF16),
            pltpu.VMEM((2, 512, 512), BF16),
            pltpu.VMEM((512, 1024), F32),
            pltpu.SemaphoreType.DMA((20,)),
            pltpu.SemaphoreType.DMA((20,)),
        ],
        compiler_params=pltpu.CompilerParams(vmem_limit_bytes=63 * 2**20),
    )(keys, fresh, moment)


def per_device(tokens, weight, momentum, gradient, indices):
    keys, fresh, moment = step(jnp.asarray(tables()), indices[0], momentum[0], gradient[0], weight, tokens)
    keys, fresh, moment = put_in_place(keys, fresh.reshape(2, 512, 512), moment)
    return (keys, fresh, moment[None])


def solution(mesh):
    return jax.shard_map(
        per_device,
        mesh=mesh,
        in_specs=(
            P(("replica", "fsdp"), None),
            P("fsdp", None),
            P("replica", "fsdp", None),
            P("replica", "fsdp", None),
            P("replica", "fsdp", None, None),
        ),
        out_specs=(P(("replica", "fsdp"), None), P("fsdp", None), P("replica", "fsdp", None)),
        check_vma=False,
    )
```
